256 devices in a mesh: depth: 2 (over z_lo), row: 8 (over x, core), col: 16 (over z_hi, y).
Axes of the slice: x: 4, y: 4, z: 8 (z_hi: 4, z_lo: 2; z = z_hi * 2 + z_lo), core: 2. Of those that a mesh axis runs over, the one named last changes fastest.
Arguments:
- normed: bfloat16 [4096, 6144], P(('depth', 'col'), 'row'), may hold values from -6 to 6
- positions: int32 [4096], P(('depth', 'col')), may hold values from 0 to 1567, as said below
- cotangent: bfloat16 [4096, 6144], P(('depth', 'col'), 'row'), may hold values from -4 to 4
- w_in: bfloat16 [6144, 12288], P('row', 'col'), may hold values from -0.078125 to 0.078125
- b_in: float32 [12288], P('col'), may hold values from -4 to 4
- w_out: bfloat16 [12288, 6144], P('col', 'row'), may hold values from -0.0546875 to 0.0546875
Outputs:
- d_normed: bfloat16 [4096, 6144], P(('depth', 'col'), 'row')
- d_w_in: float32 [6144, 12288], P('row', 'col')
- d_b_in: float32 [12288], P('col')
- d_w_out: float32 [12288, 6144], P('col', 'row')
The draws below stay inside these ranges and needn't reach their ends.
Inputs may be any that keep to these rules, and one draw needn't show every extreme that they name: positions holds 16 clips of 256 consecutive tokens; in each clip the same 256 // 8 of the 196 spatial places (ascending, always including places 0 and 195) are kept in each of the 8 frames, position = frame * 196 + place, frames ascending.
All inputs are finite; a program needn't handle non-finite values.
Results may differ from the reference program's by a relative error of at most 0.03.
Values may be sent and summed in bfloat16 or wider, within the bound.
No kernel may reach another device: no remote copies, remote signals or barrier semaphores. Data moves between devices by JAX's collectives and lax.ppermute only.
A program may use at most 128 MiB of HBM per device.

```python
import jax
import jax.numpy as jnp
from jax import lax

D = 6144
FF = 12288
VIS = 256
TOKENS = 4096
N_COL = 16


def draw_positions(key, part):
    key = jax.random.fold_in(key, 7)
    keep = VIS // 8
    clip_keys = jax.random.split(key, TOKENS // VIS)

    def one_clip(clip_key):
        inner = (jax.random.permutation(clip_key, 194)[:keep - 2] + 1).astype(jnp.int32)
        ends = jnp.array([0, 195], dtype=jnp.int32)
        chosen = jnp.sort(jnp.concatenate([ends, inner])).astype(jnp.int32)
        frames = jnp.arange(8, dtype=jnp.int32)[:, None] * 196
        return (frames + chosen[None, :]).reshape(-1)
    return jax.vmap(one_clip)(clip_keys).reshape(-1).astype(jnp.int32)


def level_of(key, extent, cuts, smallest, high):
    factor_of = 1.0
    for axis_at, parts in cuts:
        steps = jax.random.uniform(jax.random.fold_in(jax.random.fold_in(key, 6), axis_at), (parts,), jnp.float32, smallest / len(cuts), high / len(cuts))
        factor_of = factor_of * jnp.repeat(jnp.exp(steps), extent[axis_at] // parts).reshape((-1,) + (1,) * (len(extent) - 1 - axis_at))
    return factor_of


def gaussian(stream_key, dims, deviation, limit, shards=(), kind=jnp.bfloat16):
    drawn = deviation * jax.random.normal(stream_key, dims, jnp.float32)
    if shards:
        drawn = drawn * level_of(stream_key, dims, shards, -0.22, 0.18)
    return jnp.clip(drawn, -limit, limit).astype(kind)


def setup_inputs(seed: int = 0) -> dict:
    key_list = jax.random.split(jax.random.key(seed), 7)
    normed = gaussian(key_list[0], (TOKENS, D), 1.0, 6.0, ((0, 32), (1, 8)))
    positions = draw_positions(jax.random.fold_in(key_list[6], 71), 0)
    cotangent = gaussian(key_list[2], (TOKENS, D), (2.0 * TOKENS ** -0.25), 4.0, ((0, 32), (1, 8)))
    w_in = gaussian(key_list[3], (D, FF), D ** -0.5, 0.078125, ((0, 8), (1, 16)))
    b_in = gaussian(key_list[4], (FF,), 1.0, 4.0, ((0, 16),), jnp.float32)
    w_out = gaussian(key_list[5], (FF, D), FF ** -0.5, 0.0546875, ((0, 16), (1, 8)))
    return dict(normed=normed, positions=positions, cotangent=cotangent, w_in=w_in, b_in=b_in, w_out=w_out)


coeff = 0.7978845608028654


def sincos(positions, first, width):
    places = positions.astype(jnp.float32)[:, None]
    column = first + jnp.arange(width, dtype=jnp.int32)
    expo = (2 * (column // 2)).astype(jnp.float32) / jnp.float32(D)
    freq = jnp.power(jnp.float32(10000.0), -expo)
    angle = places * freq[None, :]
    return jnp.where((column % 2 == 0)[None, :], jnp.sin(angle), jnp.cos(angle))


def gelu_pair(value):
    inner = coeff * (value + 0.044715 * value * value * value)
    slope = jnp.tanh(inner)
    out = 0.5 * value * (1.0 + slope)
    grad = 0.5 * (1.0 + slope) + 0.5 * value * (1.0 - slope * slope) * coeff * (1.0 + 3.0 * 0.044715 * value * value)
    return out, grad


def reference(normed, positions, cotangent, w_in, b_in, w_out):
    inputs = (normed.astype(jnp.float32) + sincos(positions, 0, D)).astype(jnp.bfloat16)
    pre = jnp.dot(inputs, w_in, preferred_element_type=jnp.float32) + b_in.astype(jnp.float32)
    act_f, slope = gelu_pair(pre)
    act = act_f.astype(jnp.bfloat16)
    d_act = jnp.dot(cotangent, w_out.T, preferred_element_type=jnp.float32)
    d_pre = (d_act * slope).astype(jnp.bfloat16)
    d_w_out = jnp.dot(act.T, cotangent, preferred_element_type=jnp.float32)
    d_w_in = jnp.dot(inputs.T, d_pre, preferred_element_type=jnp.float32)
    d_b_in = jnp.sum(d_pre.astype(jnp.float32), axis=0)
    block = FF // N_COL
    grad_blocks = d_pre.reshape(TOKENS, N_COL, block).transpose(1, 0, 2)
    weight_blocks = w_in.reshape(D, N_COL, block).transpose(1, 0, 2)

    def add_block(total, pair):
        part = jnp.dot(pair[0], pair[1].T, preferred_element_type=jnp.float32).astype(jnp.bfloat16)
        return total + part.astype(jnp.float32), None

    total, unused = lax.scan(add_block, jnp.zeros((TOKENS, D), jnp.float32), (grad_blocks, weight_blocks))
    d_normed = total.astype(jnp.bfloat16)
    return d_normed, d_w_in, d_b_in, d_w_out
```

```python
import jax
import jax.numpy as jnp
from jax import lax
from jax.sharding import PartitionSpec as P

D = 6144
AXES = ("depth", "row", "col")

coeff = 0.7978845608028654


def sincos(positions, first, width):
    places = positions.astype(jnp.float32)[:, None]
    column = first + jnp.arange(width, dtype=jnp.int32)
    expo = (2 * (column // 2)).astype(jnp.float32) / jnp.float32(D)
    freq = jnp.power(jnp.float32(10000.0), -expo)
    angle = places * freq[None, :]
    return jnp.where((column % 2 == 0)[None, :], jnp.sin(angle), jnp.cos(angle))


def gelu_pair(value):
    inner = coeff * (value + 0.044715 * value * value * value)
    slope = jnp.tanh(inner)
    out = 0.5 * value * (1.0 + slope)
    grad = 0.5 * (1.0 + slope) + 0.5 * value * (1.0 - slope * slope) * coeff * (
        1.0 + 3.0 * 0.044715 * value * value
    )
    return (out, grad)


def moves(shift):
    def index(d, x, c, z, y):
        return ((d % 2) * 8 + (x % 4) * 2 + c % 2) * 16 + (z % 4) * 4 + y % 4

    return [
        (index(d, x, c, z, y), index(*shift(d, x, c, z, y)))
        for d in range(2)
        for x in range(4)
        for c in range(2)
        for z in range(4)
        for y in range(4)
    ]


CORE = moves(lambda d, x, c, z, y: (d, x, c + 1, z, y))
DEPTH = moves(lambda d, x, c, z, y: (d + 1, x, c, z, y))
X_BY = [moves(lambda d, x, c, z, y, s=s: (d, x + s, c, z, y)) for s in range(4)]
Y_BY = [moves(lambda d, x, c, z, y, k=k: (d, x, c, z, y + k)) for k in range(4)]
Z_GATHER = [moves(lambda d, x, c, z, y, s=s: (d, x, c, z - x - s, y)) for s in range(4)]
Z_SCATTER = [moves(lambda d, x, c, z, y, s=s: (d, x, c, z + x + s, y)) for s in range(4)]

GROUPS = ((0, 1, 3), (2,))


def send(value, pairs):
    return lax.ppermute(value, AXES, pairs)


def dot(a, b, contract, kind=jnp.float32):
    return lax.dot_general(
        a, b, ((contract[:1], contract[1:]), ((), ())), preferred_element_type=jnp.float32
    ).astype(kind)


def on_device(normed, positions, cotangent, w_in, b_in, w_out):
    bf, f32 = jnp.bfloat16, jnp.float32
    width = w_in.shape[0]
    hidden = w_in.shape[1]
    row = lax.axis_index("row")
    core = row % 2
    half = normed.shape[0] // 2

    def split(value):
        mine = lax.dynamic_slice_in_dim(value, core * half, half, 0)
        other = lax.dynamic_slice_in_dim(value, (1 - core) * half, half, 0)
        return mine, other

    def widen(value):
        mine, other = split(value)
        return jnp.concatenate([mine, send(other, CORE)], axis=1)

    inputs = (normed.astype(f32) + sincos(positions, row * width, width)).astype(bf)
    x_half = widen(inputs)
    c_half = widen(cotangent)
    w_in_all = jnp.concatenate([w_in, send(w_in, CORE)], axis=0)
    w_out_all = jnp.concatenate([w_out, send(w_out, CORE)], axis=1)

    def gather(value):
        own = jnp.concatenate([send(value, Z_GATHER[s]) for s in range(4)], axis=0)
        return [own] + [send(own, Y_BY[(4 - k) % 4]) for k in range(1, 4)]

    x_parts = gather(x_half)
    c_parts = gather(c_half)

    def grouped(parts, group):
        return parts[group[0]] if len(group) == 1 else jnp.concatenate([parts[k] for k in group], axis=0)

    def scatter_x(part, n):
        part = part.reshape(n, 4, half, hidden)
        total = part[:, 0].astype(f32)
        for s in range(1, 4):
            total = total + send(part[:, s], X_BY[s]).astype(f32)
        return total

    def gather_x(own):
        got = [own] + [send(own, X_BY[4 - s]) for s in range(1, 4)]
        return jnp.stack(got, axis=1).reshape(-1, hidden)

    xs = [grouped(x_parts, g) for g in GROUPS]
    cs = [grouped(c_parts, g) for g in GROUPS]
    acts, slopes, d_pres = [], [], []
    for g, value in zip(GROUPS, xs):
        pre = scatter_x(dot(value, w_in_all, (1, 0), bf), len(g)) + b_in[None, None, :]
        act, slope = gelu_pair(pre)
        acts.append(gather_x(act.astype(bf)))
        slopes.append(slope)
    for g, value, slope in zip(GROUPS, cs, slopes):
        d_act = scatter_x(dot(value, w_out_all, (1, 1), bf), len(g))
        d_pres.append(gather_x((d_act * slope).astype(bf)))

    def weight_grad(lefts, rights):
        out = None
        for a, b in zip(lefts, rights):
            term = dot(a, b, (0, 0))
            out = term if out is None else out + term
        return out

    out_other = weight_grad(acts, [c[:, width:] for c in cs]).astype(bf)
    out_got = send(out_other, CORE)
    out_mine = (weight_grad(acts, [c[:, :width] for c in cs]) + out_got.astype(f32)).astype(bf)
    d_w_out = out_mine.astype(f32) + send(out_mine, DEPTH).astype(f32)

    in_other = weight_grad([x[:, width:] for x in xs], d_pres).astype(bf)
    in_got = send(in_other, CORE)
    in_mine = (weight_grad([x[:, :width] for x in xs], d_pres) + in_got.astype(f32)).astype(bf)
    d_w_in = in_mine.astype(f32) + send(in_mine, DEPTH).astype(f32)

    bias = jnp.zeros((4, hidden), f32)
    for d_pre in d_pres:
        bias = bias + jnp.sum(d_pre.reshape(-1, 4, half, hidden).astype(f32), axis=(0, 2))
    bias = ((bias[0] + bias[2]) + (bias[1] + bias[3]))[None]
    bias = bias + send(bias, CORE)
    bias = bias + send(bias, DEPTH)
    d_b_in = bias[0]

    total = None
    for g, d_pre in zip(GROUPS, d_pres):
        part = dot(d_pre, w_in_all, (1, 1), bf).reshape(len(g), 4 * half, 2 * width)
        for i, k in enumerate(g):
            term = (part[i] if k == 0 else send(part[i], Y_BY[k])).astype(f32)
            total = term if total is None else total + term
    total = total.astype(bf).reshape(4, half, 2 * width)
    d_half = None
    for s in range(4):
        term = send(total[s], Z_SCATTER[s]).astype(f32)
        d_half = term if d_half is None else d_half + term
    d_half = d_half.astype(bf)
    mine, got = d_half[:, :width], send(d_half[:, width:], CORE)
    first = jnp.where(core == 0, mine, got)
    second = jnp.where(core == 0, got, mine)
    d_normed = jnp.concatenate([first, second], axis=0)
    return (d_normed, d_w_in, d_b_in, d_w_out)


def solution(mesh):
    placed = (
        P(("depth", "col"), "row"),
        P(("depth", "col")),
        P(("depth", "col"), "row"),
        P("row", "col"),
        P("col"),
        P("col", "row"),
    )
    return jax.shard_map(
        on_device,
        mesh=mesh,
        in_specs=placed,
        out_specs=(P(("depth", "col"), "row"), P("row", "col"), P("col"), P("col", "row")),
        check_vma=False,
    )
```

```python
import jax
import jax.numpy as jnp
from jax import lax
from jax.sharding import PartitionSpec as P

D = 6144
AXES = ("depth", "row", "col")

coeff = 0.7978845608028654


def sincos(positions, first, width):
    places = positions.astype(jnp.float32)[:, None]
    column = first + jnp.arange(width, dtype=jnp.int32)
    expo = (2 * (column // 2)).astype(jnp.float32) / jnp.float32(D)
    freq = jnp.power(jnp.float32(10000.0), -expo)
    angle = places * freq[None, :]
    return jnp.where((column % 2 == 0)[None, :], jnp.sin(angle), jnp.cos(angle))


def gelu_pair(value):
    inner = coeff * (value + 0.044715 * value * value * value)
    slope = jnp.tanh(inner)
    out = 0.5 * value * (1.0 + slope)
    grad = 0.5 * (1.0 + slope) + 0.5 * value * (1.0 - slope * slope) * coeff * (
        1.0 + 3.0 * 0.044715 * value * value
    )
    return (out, grad)


def moves(shift):
    def index(d, x, c, z, y):
        return ((d % 2) * 8 + (x % 4) * 2 + c % 2) * 16 + (z % 4) * 4 + y % 4

    return [
        (index(d, x, c, z, y), index(*shift(d, x, c, z, y)))
        for d in range(2)
        for x in range(4)
        for c in range(2)
        for z in range(4)
        for y in range(4)
    ]


CORE = moves(lambda d, x, c, z, y: (d, x, c + 1, z, y))
DEPTH = moves(lambda d, x, c, z, y: (d + 1, x, c, z, y))
X_BY = [moves(lambda d, x, c, z, y, s=s: (d, x + s, c, z, y)) for s in range(4)]
Y_BY = [moves(lambda d, x, c, z, y, k=k: (d, x, c, z, y + k)) for k in range(4)]
Z_GATHER = [moves(lambda d, x, c, z, y, s=s: (d, x, c, z - x - s, y)) for s in range(4)]
Z_SCATTER = [moves(lambda d, x, c, z, y, s=s: (d, x, c, z + x + s, y)) for s in range(4)]

GROUPS = ((0, 1, 3), (2,))


def send(value, pairs):
    return lax.ppermute(value, AXES, pairs)


def dot(a, b, contract, kind=jnp.float32):
    return lax.dot_general(
        a, b, ((contract[:1], contract[1:]), ((), ())), preferred_element_type=jnp.float32
    ).astype(kind)


def on_device(normed, positions, cotangent, w_in, b_in, w_out):
    bf, f32 = jnp.bfloat16, jnp.float32
    width = w_in.shape[0]
    hidden = w_in.shape[1]
    row = lax.axis_index("row")
    core = row % 2
    half = normed.shape[0] // 2

    def split(value):
        mine = lax.dynamic_slice_in_dim(value, core * half, half, 0)
        other = lax.dynamic_slice_in_dim(value, (1 - core) * half, half, 0)
        return mine, other

    def widen(value):
        mine, other = split(value)
        return jnp.concatenate([mine, send(other, CORE)], axis=1)

    def after(value, *others):
        return lax.optimization_barrier((value, *others))[0]

    inputs = (normed.astype(f32) + sincos(positions, row * width, width)).astype(bf)
    x_half = widen(inputs)
    c_half = widen(cotangent)
    w_in_all = jnp.concatenate([w_in, send(after(w_in, x_half), CORE)], axis=0)
    w_out_all = jnp.concatenate([w_out, send(after(w_out, x_half), CORE)], axis=1)

    def gather_z(value):
        return jnp.concatenate([send(value, Z_GATHER[s]) for s in range(4)], axis=0)

    def gather_y(own):
        up, down = send(own, Y_BY[3]), send(own, Y_BY[1])
        return up, down

    def far(up, down):
        return jnp.concatenate([send(up[:, :width], Y_BY[3]), send(down[:, width:], Y_BY[1])], axis=1)

    x_own = gather_z(x_half)
    c_own = gather_z(after(c_half, x_own))
    x_up, x_down = gather_y(x_own)
    x_far = far(x_up, x_down)
    c_up, c_down = gather_y(after(c_own, x_up, x_down))
    x_parts = [x_own, x_up, x_far, x_down]

    def grouped(parts, group):
        return parts[group[0]] if len(group) == 1 else jnp.concatenate([parts[k] for k in group], axis=0)

    def scatter_x(part, n):
        part = part.reshape(n, 4, half, hidden)
        total = part[:, 0].astype(f32)
        for s in range(1, 4):
            total = total + send(part[:, s], X_BY[s]).astype(f32)
        return total

    def gather_x(own):
        got = [own] + [send(own, X_BY[4 - s]) for s in range(1, 4)]
        return jnp.stack(got, axis=1).reshape(-1, hidden)

    xs = [grouped(x_parts, g) for g in GROUPS]
    acts, slopes, d_pres = [], [], []
    parts = [dot(value, w_in_all, (1, 0), bf) for value in xs]
    for g, part in zip(GROUPS, parts):
        pre = scatter_x(part, len(g)) + b_in[None, None, :]
        act, slope = gelu_pair(pre)
        acts.append(act.astype(bf))
        slopes.append(slope)
    acts = [gather_x(act) for act in acts]
    c_up, c_down = after(c_up, parts[0], parts[1]), after(c_down, parts[0], parts[1])
    c_far = far(c_up, c_down)
    c_parts = [c_own, c_up, c_far, c_down]
    cs = [grouped(c_parts, g) for g in GROUPS]
    for g, value, slope in zip(GROUPS, cs, slopes):
        d_act = scatter_x(dot(value, w_out_all, (1, 1), bf), len(g))
        d_pres.append(gather_x((d_act * slope).astype(bf)))

    def weight_grad(lefts, rights):
        out = None
        for a, b in zip(lefts, rights):
            term = dot(a, b, (0, 0))
            out = term if out is None else out + term
        return out

    out_other = weight_grad(acts, [c[:, width:] for c in cs]).astype(bf)
    out_got = send(out_other, CORE)
    out_mine = (weight_grad(acts, [c[:, :width] for c in cs]) + out_got.astype(f32)).astype(bf)
    d_w_out = out_mine.astype(f32) + send(out_mine, DEPTH).astype(f32)

    in_other = weight_grad([x[:, width:] for x in xs], d_pres).astype(bf)
    in_got = send(in_other, CORE)
    in_mine = (weight_grad([x[:, :width] for x in xs], d_pres) + in_got.astype(f32)).astype(bf)
    d_w_in = in_mine.astype(f32) + send(in_mine, DEPTH).astype(f32)

    bias = jnp.zeros((4, hidden), f32)
    for d_pre in d_pres:
        bias = bias + jnp.sum(d_pre.reshape(-1, 4, half, hidden).astype(f32), axis=(0, 2))
    bias = ((bias[0] + bias[2]) + (bias[1] + bias[3]))[None]
    bias = bias + send(bias, CORE)
    bias = bias + send(bias, DEPTH)
    d_b_in = bias[0]

    total = None
    for g, d_pre in zip(GROUPS, d_pres):
        part = dot(d_pre, w_in_all, (1, 1), bf).reshape(len(g), 4 * half, 2 * width)
        for i, k in enumerate(g):
            term = (part[i] if k == 0 else send(part[i], Y_BY[k])).astype(f32)
            total = term if total is None else total + term
    total = total.astype(bf).reshape(4, half, 2 * width)
    d_half = None
    for s in range(4):
        term = send(total[s], Z_SCATTER[s]).astype(f32)
        d_half = term if d_half is None else d_half + term
    d_half = d_half.astype(bf)
    mine, got = d_half[:, :width], send(d_half[:, width:], CORE)
    first = jnp.where(core == 0, mine, got)
    second = jnp.where(core == 0, got, mine)
    d_normed = jnp.concatenate([first, second], axis=0)
    return (d_normed, d_w_in, d_b_in, d_w_out)


def solution(mesh):
    placed = (
        P(("depth", "col"), "row"),
        P(("depth", "col")),
        P(("depth", "col"), "row"),
        P("row", "col"),
        P("col"),
        P("col", "row"),
    )
    return jax.shard_map(
        on_device,
        mesh=mesh,
        in_specs=placed,
        out_specs=(P(("depth", "col"), "row"), P("row", "col"), P("col"), P("col", "row")),
        check_vma=False,
    )
```

```python
import jax
import jax.numpy as jnp
from jax import lax
from jax.sharding import PartitionSpec as P

D = 6144
AXES = ("depth", "row", "col")

coeff = 0.7978845608028654


def sincos(positions, first, width):
    places = positions.astype(jnp.float32)[:, None]
    column = first + jnp.arange(width, dtype=jnp.int32)
    expo = (2 * (column // 2)).astype(jnp.float32) / jnp.float32(D)
    freq = jnp.power(jnp.float32(10000.0), -expo)
    angle = places * freq[None, :]
    return jnp.where((column % 2 == 0)[None, :], jnp.sin(angle), jnp.cos(angle))


def gelu_pair(value):
    inner = coeff * (value + 0.044715 * value * value * value)
    slope = jnp.tanh(inner)
    out = 0.5 * value * (1.0 + slope)
    grad = 0.5 * (1.0 + slope) + 0.5 * value * (1.0 - slope * slope) * coeff * (
        1.0 + 3.0 * 0.044715 * value * value
    )
    return (out, grad)


def moves(shift):
    def index(d, x, c, z, y):
        return ((d % 2) * 8 + (x % 4) * 2 + c % 2) * 16 + (z % 4) * 4 + y % 4

    return [
        (index(d, x, c, z, y), index(*shift(d, x, c, z, y)))
        for d in range(2)
        for x in range(4)
        for c in range(2)
        for z in range(4)
        for y in range(4)
    ]


CORE = moves(lambda d, x, c, z, y: (d, x, c + 1, z, y))
DEPTH = moves(lambda d, x, c, z, y: (d + 1, x, c, z, y))
Y_BY = [moves(lambda d, x, c, z, y, k=k: (d, x, c, z, y + k)) for k in range(4)]
Z_BY = [moves(lambda d, x, c, z, y, j=j: (d, x, c, z + j, y)) for j in range(4)]
X_SETS = [[c + 2 * x for x in range(4)] for c in range(2)]

IN_GROUPS = ((0,), (1, 3), (2,))
OUT_GROUPS = ((0, 1, 3), (2,))


def send(value, pairs):
    return lax.ppermute(value, AXES, pairs)


def dot(a, b, contract, kind=jnp.float32):
    return lax.dot_general(
        a, b, ((contract[:1], contract[1:]), ((), ())), preferred_element_type=jnp.float32
    ).astype(kind)


def on_device(normed, positions, cotangent, w_in, b_in, w_out):
    bf, f32 = jnp.bfloat16, jnp.float32
    width = w_in.shape[0]
    hidden = w_in.shape[1]
    row = lax.axis_index("row")
    core = row % 2
    half = normed.shape[0] // 2

    def after(value, *others):
        return lax.optimization_barrier((value, *others))[0]

    def gather_z(value):
        return jnp.concatenate([value] + [send(value, Z_BY[4 - j]) for j in range(1, 4)], axis=0)

    def far(up, down):
        return jnp.concatenate([send(up[:, :width], Y_BY[3]), send(down[:, width:], Y_BY[1])], axis=1)

    def swap_x(value):
        return lax.all_to_all(value, "row", 1, 1, tiled=True, axis_index_groups=X_SETS)

    def scatter_x(parts):
        part = jnp.stack(parts).reshape(len(parts), 4, half, hidden)
        return jnp.sum(swap_x(part).astype(f32), axis=1)

    def gather_x(own):
        return swap_x(jnp.broadcast_to(own[:, None], (own.shape[0], 4, half, hidden))).reshape(-1, 4 * half, hidden)

    inputs = (normed.astype(f32) + sincos(positions, row * width, width)).astype(bf)
    both = jnp.stack([inputs, cotangent])
    mine = lax.dynamic_slice_in_dim(both, core * half, half, 1)
    other = send(lax.dynamic_slice_in_dim(both, (1 - core) * half, half, 1), CORE)
    x_half = jnp.concatenate([mine[0], other[0]], axis=1)
    c_half = jnp.concatenate([mine[1], other[1]], axis=1)
    w_in_got = send(w_in, CORE)
    w_out_got = send(w_out, CORE)
    w_in_all = jnp.concatenate([w_in, w_in_got], axis=0)
    w_out_all = jnp.concatenate([w_out, w_out_got], axis=1)

    x_own = gather_z(x_half)
    x_up, x_down = send(x_own, Y_BY[3]), send(x_own, Y_BY[1])
    c_own = gather_z(after(c_half, x_own, w_in_got, w_out_got))
    xs = [x_own, x_up, None, x_down]
    parts = [dot(x_own, w_in_all, (1, 0), bf), None, None, None]
    x_up_2, x_down_2 = after((x_up, x_down), parts[0])
    xs[1], xs[3] = x_up_2, x_down_2
    xs[2] = far(x_up_2, x_down_2)
    c_own = after(c_own, x_up_2, x_down_2)
    c_up, c_down = send(c_own, Y_BY[3]), send(c_own, Y_BY[1])
    for k in (1, 3, 2):
        parts[k] = dot(xs[k], w_in_all, (1, 0), bf)

    acts, slopes = {}, {}
    for g in IN_GROUPS:
        pre = scatter_x([parts[k] for k in g]) + b_in[None, None, :]
        act, slope = gelu_pair(pre)
        for i, k in enumerate(g):
            acts[k], slopes[k] = act[i], slope[i]
    order = (0, 1, 3, 2)
    act_all = gather_x(jnp.stack([acts[k] for k in order]).astype(bf))
    acts = {k: act_all[i] for i, k in enumerate(order)}

    c_up, c_down = after((c_up, c_down), parts[2])
    cs = [c_own, c_up, far(c_up, c_down), c_down]
    d_pres = {}
    for g in OUT_GROUPS:
        d_act = scatter_x([dot(cs[k], w_out_all, (1, 1), bf) for k in g])
        d_pre = gather_x((d_act * jnp.stack([slopes[k] for k in g])).astype(bf))
        for i, k in enumerate(g):
            d_pres[k] = d_pre[i]
    acts = [acts[k] for k in range(4)]
    d_pres = [d_pres[k] for k in range(4)]

    def weight_grad(lefts, rights):
        out = None
        for a, b in zip(lefts, rights):
            term = dot(a, b, (0, 0))
            out = term if out is None else out + term
        return out

    out_other = weight_grad(acts, [c[:, width:] for c in cs]).astype(bf)
    out_got = send(out_other, CORE)
    out_mine = (weight_grad(acts, [c[:, :width] for c in cs]) + out_got.astype(f32)).astype(bf)
    d_w_out = out_mine.astype(f32) + send(out_mine, DEPTH).astype(f32)

    in_other = weight_grad([x[:, width:] for x in xs], d_pres).astype(bf)
    in_got = send(in_other, CORE)
    in_mine = (weight_grad([x[:, :width] for x in xs], d_pres) + in_got.astype(f32)).astype(bf)
    d_w_in = in_mine.astype(f32) + send(in_mine, DEPTH).astype(f32)

    bias = jnp.zeros((4, hidden), f32)
    for d_pre in d_pres:
        bias = bias + jnp.sum(d_pre.reshape(4, half, hidden).astype(f32), axis=1)
    bias = ((bias[0] + bias[2]) + (bias[1] + bias[3]))[None]
    bias = bias + send(bias, CORE)
    bias = bias + send(bias, DEPTH)
    d_b_in = bias[0]

    total = dot(d_pres[0], w_in_all, (1, 1))
    for k in (1, 3, 2):
        total = total + send(dot(d_pres[k], w_in_all, (1, 1), bf), Y_BY[k]).astype(f32)
    total = total.reshape(4, half, 2 * width)
    d_half = total[0]
    for j in range(1, 4):
        d_half = d_half + send(total[j].astype(bf), Z_BY[j]).astype(f32)
    d_half = d_half.astype(bf)
    mine, got = d_half[:, :width], send(d_half[:, width:], CORE)
    first = jnp.where(core == 0, mine, got)
    second = jnp.where(core == 0, got, mine)
    d_normed = jnp.concatenate([first, second], axis=0)
    return (d_normed, d_w_in, d_b_in, d_w_out)


def solution(mesh):
    placed = (
        P(("depth", "col"), "row"),
        P(("depth", "col")),
        P(("depth", "col"), "row"),
        P("row", "col"),
        P("col"),
        P("col", "row"),
    )
    return jax.shard_map(
        on_device,
        mesh=mesh,
        in_specs=placed,
        out_specs=(P(("depth", "col"), "row"), P("row", "col"), P("col"), P("col", "row")),
        check_vma=False,
    )
```

```python
import jax
import jax.numpy as jnp
from jax import lax
from jax.sharding import PartitionSpec as P

D = 6144
AXES = ("depth", "row", "col")

coeff = 0.7978845608028654


def sincos(positions, first, width):
    places = positions.astype(jnp.float32)[:, None]
    column = first + jnp.arange(width, dtype=jnp.int32)
    expo = (2 * (column // 2)).astype(jnp.float32) / jnp.float32(D)
    freq = jnp.power(jnp.float32(10000.0), -expo)
    angle = places * freq[None, :]
    return jnp.where((column % 2 == 0)[None, :], jnp.sin(angle), jnp.cos(angle))


def gelu_pair(value):
    inner = coeff * (value + 0.044715 * value * value * value)
    slope = jnp.tanh(inner)
    out = 0.5 * value * (1.0 + slope)
    grad = 0.5 * (1.0 + slope) + 0.5 * value * (1.0 - slope * slope) * coeff * (
        1.0 + 3.0 * 0.044715 * value * value
    )
    return (out, grad)


def moves(shift):
    def index(d, x, c, z, y):
        return ((d % 2) * 8 + (x % 4) * 2 + c % 2) * 16 + (z % 4) * 4 + y % 4

    return [
        (index(d, x, c, z, y), index(*shift(d, x, c, z, y)))
        for d in range(2)
        for x in range(4)
        for c in range(2)
        for z in range(4)
        for y in range(4)
    ]


CORE = moves(lambda d, x, c, z, y: (d, x, c + 1, z, y))
DEPTH = moves(lambda d, x, c, z, y: (d + 1, x, c, z, y))
Y_BY = [moves(lambda d, x, c, z, y, k=k: (d, x, c, z, y + k)) for k in range(4)]
Z_BY = [moves(lambda d, x, c, z, y, j=j: (d, x, c, z + j, y)) for j in range(4)]
X_SETS = [[c + 2 * x for x in range(4)] for c in range(2)]

Y_SETS = [[z * 4 + y for y in range(4)] for z in range(4)]
IN_GROUPS = ((0, 1, 3), (2,))


def send(value, pairs):
    return lax.ppermute(value, AXES, pairs)


def dot(a, b, contract, kind=jnp.float32):
    return lax.dot_general(
        a, b, ((contract[:1], contract[1:]), ((), ())), preferred_element_type=jnp.float32
    ).astype(kind)


def on_device(normed, positions, cotangent, w_in, b_in, w_out):
    bf, f32 = jnp.bfloat16, jnp.float32
    width = w_in.shape[0]
    hidden = w_in.shape[1]
    row = lax.axis_index("row")
    core = row % 2
    half = normed.shape[0] // 2

    def after(value, *others):
        return lax.optimization_barrier((value, *others))[0]

    def gather_z(value):
        return jnp.concatenate([value] + [send(value, Z_BY[4 - j]) for j in range(1, 4)], axis=0)

    def swap_x(value):
        return lax.all_to_all(value, "row", 0, 0, tiled=True, axis_index_groups=X_SETS)

    def scatter_x(part):
        return jnp.sum(swap_x(part).astype(f32), axis=0)

    def gather_x(own):
        return swap_x(jnp.broadcast_to(own[None], (4,) + own.shape))

    inputs = (normed.astype(f32) + sincos(positions, row * width, width)).astype(bf)
    both = jnp.stack([inputs, cotangent])
    mine = lax.dynamic_slice_in_dim(both, core * half, half, 1)
    other = send(lax.dynamic_slice_in_dim(both, (1 - core) * half, half, 1), CORE)
    x_half = jnp.concatenate([mine[0], other[0]], axis=1)
    c_half = jnp.concatenate([mine[1], other[1]], axis=1)
    w_in_got = send(w_in, CORE)
    w_out_got = send(w_out, CORE)
    w_in_all = jnp.concatenate([w_in, w_in_got], axis=0)
    w_out_all = jnp.concatenate([w_out, w_out_got], axis=1)

    x_own = gather_z(x_half)
    c_four = lax.all_to_all(
        jnp.broadcast_to(c_half[None], (4,) + c_half.shape), "col", 0, 0, tiled=True, axis_index_groups=Y_SETS
    )
    y = lax.axis_index("col") % 4
    c_own = lax.dynamic_slice_in_dim(jnp.concatenate([c_four, c_four]), y, 4, 0)

    x_own = after(x_own, c_four)
    x_up, x_down = send(x_own, Y_BY[3]), send(x_own, Y_BY[1])
    c_own = after(c_own, x_own, w_in_got, w_out_got)
    c_up, c_down = send(c_own, Z_BY[3]), send(c_own, Z_BY[1])
    xs = [x_own, x_up, None, x_down]
    parts = [dot(x_own, w_in_all, (1, 0), bf), None, None, None]
    x_up, x_down = after((x_up, x_down), parts[0])
    rows = 2 * half
    xs[1], xs[3] = x_up, x_down
    xs[2] = jnp.concatenate([send(x_up[:rows], Y_BY[3]), send(x_down[rows:], Y_BY[1])])
    acts, slopes = [None] * 4, [None] * 4
    pre = None
    for g in IN_GROUPS:
        for k in g:
            if parts[k] is None:
                parts[k] = dot(xs[k], w_in_all, (1, 0), bf)
        part = jnp.stack([parts[k].reshape(4, half, hidden) for k in g], axis=1)
        pre = scatter_x(part if pre is None else after(part, pre)) + b_in[None, None, :]
        act, slope = gelu_pair(pre)
        for i, k in enumerate(g):
            acts[k], slopes[k] = act[i], slope[i]
    act_all = gather_x(jnp.stack(acts).astype(bf))

    c_up, c_down = after((c_up, c_down), parts[2])
    c_far = jnp.concatenate([send(c_up[:2], Z_BY[3]), send(c_down[2:], Z_BY[1])])
    cs = [c.reshape(-1, 2 * width) for c in (c_own, c_up, c_far, c_down)]
    d_parts = jnp.stack([dot(c, w_out_all, (1, 1), bf).reshape(4, half, hidden) for c in cs])
    d_act = scatter_x(after(d_parts, act_all))
    d_pre_all = gather_x((d_act * jnp.stack(slopes)).astype(bf))

    act_all = act_all.reshape(-1, hidden)
    c_mine = jnp.concatenate([c[:, :width] for c in cs])
    c_other = jnp.concatenate([c[:, width:] for c in cs])
    out_got = send(dot(act_all, c_other, (0, 0), bf), CORE)
    out_mine = (dot(act_all, c_mine, (0, 0)) + out_got.astype(f32)).astype(bf)
    out_deep = send(out_mine, DEPTH)
    d_w_out = out_mine.astype(f32) + out_deep.astype(f32)

    d_pre_all = after(d_pre_all, out_mine).swapaxes(0, 1)
    d_pres = [d_pre_all[k].reshape(4 * half, hidden) for k in range(4)]
    shares = [dot(d_pres[k], w_in_all, (1, 1), bf) for k in (1, 3, 2)]
    d_pre_all = after(d_pre_all, out_deep, *shares)
    d_pre_rows = d_pre_all.reshape(-1, hidden)
    x_mine = jnp.concatenate([x[:, :width] for x in xs])
    x_other = jnp.concatenate([x[:, width:] for x in xs])
    x_other = jnp.concatenate([x_other, jnp.ones((x_other.shape[0], 16), bf)], axis=1)
    in_other = dot(x_other, d_pre_rows, (0, 0), bf)
    in_got = send(in_other, CORE)
    in_mine = (dot(x_mine, d_pre_rows, (0, 0)) + in_got[:width].astype(f32)).astype(bf)
    bias = (in_other[width:].astype(f32) + in_got[width:].astype(f32)).astype(bf)
    in_mine = jnp.concatenate([in_mine, bias])
    d_in = in_mine.astype(f32) + send(in_mine, DEPTH).astype(f32)
    d_w_in, d_b_in = d_in[:width], d_in[width]

    total = dot(d_pres[0], w_in_all, (1, 1))
    for k, share in zip((1, 3, 2), shares):
        total = total + send(share, Y_BY[k]).astype(f32)
    total = total.reshape(4, half, 2 * width)
    d_half = total[0]
    for j in range(1, 4):
        d_half = d_half + send(total[j].astype(bf), Z_BY[j]).astype(f32)
    d_half = d_half.astype(bf)
    mine, got = d_half[:, :width], send(d_half[:, width:], CORE)
    first = jnp.where(core == 0, mine, got)
    second = jnp.where(core == 0, got, mine)
    d_normed = jnp.concatenate([first, second], axis=0)
    return (d_normed, d_w_in, d_b_in, d_w_out)


def solution(mesh):
    placed = (
        P(("depth", "col"), "row"),
        P(("depth", "col")),
        P(("depth", "col"), "row"),
        P("row", "col"),
        P("col"),
        P("col", "row"),
    )
    return jax.shard_map(
        on_device,
        mesh=mesh,
        in_specs=placed,
        out_specs=(P(("depth", "col"), "row"), P("row", "col"), P("col"), P("col", "row")),
        check_vma=False,
    )
```

```python
import jax
import jax.numpy as jnp
from jax import lax
from jax.sharding import PartitionSpec as P

D = 6144
AXES = ("depth", "row", "col")

coeff = 0.7978845608028654


def sincos(positions, first, width):
    places = positions.astype(jnp.float32)[:, None]
    column = first + jnp.arange(width, dtype=jnp.int32)
    expo = (2 * (column // 2)).astype(jnp.float32) / jnp.float32(D)
    freq = jnp.power(jnp.float32(10000.0), -expo)
    angle = places * freq[None, :]
    return jnp.where((column % 2 == 0)[None, :], jnp.sin(angle), jnp.cos(angle))


def gelu_pair(value):
    inner = coeff * (value + 0.044715 * value * value * value)
    slope = jnp.tanh(inner)
    out = 0.5 * value * (1.0 + slope)
    grad = 0.5 * (1.0 + slope) + 0.5 * value * (1.0 - slope * slope) * coeff * (
        1.0 + 3.0 * 0.044715 * value * value
    )
    return (out, grad)


def moves(shift):
    def index(d, x, c, z, y):
        return ((d % 2) * 8 + (x % 4) * 2 + c % 2) * 16 + (z % 4) * 4 + y % 4

    return [
        (index(d, x, c, z, y), index(*shift(d, x, c, z, y)))
        for d in range(2)
        for x in range(4)
        for c in range(2)
        for z in range(4)
        for y in range(4)
    ]


CORE = moves(lambda d, x, c, z, y: (d, x, c + 1, z, y))
DEPTH = moves(lambda d, x, c, z, y: (d + 1, x, c, z, y))
Y_BY = [moves(lambda d, x, c, z, y, k=k: (d, x, c, z, y + k)) for k in range(4)]
Z_BY = [moves(lambda d, x, c, z, y, j=j: (d, x, c, z + j, y)) for j in range(4)]
X_SETS = [[c + 2 * x for x in range(4)] for c in range(2)]

Y_SETS = [[z * 4 + y for y in range(4)] for z in range(4)]


def send(value, pairs):
    return lax.ppermute(value, AXES, pairs)


def dot(a, b, contract, kind=jnp.float32):
    return lax.dot_general(
        a, b, ((contract[:1], contract[1:]), ((), ())), preferred_element_type=jnp.float32
    ).astype(kind)


def on_device(normed, positions, cotangent, w_in, b_in, w_out):
    bf, f32 = jnp.bfloat16, jnp.float32
    width = w_in.shape[0]
    hidden = w_in.shape[1]
    row = lax.axis_index("row")
    core = row % 2
    half = normed.shape[0] // 2

    def after(value, *others):
        return lax.optimization_barrier((value, *others))[0]

    def swap_x(value):
        return lax.all_to_all(value, "row", 0, 0, tiled=True, axis_index_groups=X_SETS)

    def scatter_x(part):
        return jnp.sum(swap_x(part).astype(f32), axis=0)

    def gather_x(own):
        return swap_x(jnp.broadcast_to(own[None], (4,) + own.shape))

    inputs = (normed.astype(f32) + sincos(positions, row * width, width)).astype(bf)
    both = jnp.stack([inputs, cotangent])
    mine = lax.dynamic_slice_in_dim(both, core * half, half, 1)
    other = send(lax.dynamic_slice_in_dim(both, (1 - core) * half, half, 1), CORE)
    x_half = jnp.concatenate([mine[0], other[0]], axis=1)
    c_half = jnp.concatenate([mine[1], other[1]], axis=1)
    w_in_got = send(w_in, CORE)
    w_out_got = send(w_out, CORE)
    w_in_all = jnp.concatenate([w_in, w_in_got], axis=0)
    w_out_all = jnp.concatenate([w_out, w_out_got], axis=1)

    x_one, x_three, x_two = (send(x_half, Z_BY[4 - j]) for j in (1, 3, 2))
    c_four = jnp.broadcast_to(after(c_half, x_half)[None], (4,) + c_half.shape)
    c_four = lax.all_to_all(c_four, "col", 0, 0, tiled=True, axis_index_groups=Y_SETS)
    y = lax.axis_index("col") % 4
    c_own = lax.dynamic_slice_in_dim(jnp.concatenate([c_four, c_four]), y, 4, 0)
    x_own = jnp.concatenate([x_half, x_one, x_two, x_three])

    x_up, x_down = send(x_own, Y_BY[3]), send(x_own, Y_BY[1])
    c_own = after(c_own, x_own, w_in_got, w_out_got)
    c_up, c_down = send(c_own, Z_BY[3]), send(c_own, Z_BY[1])
    parts = [dot(x_own, w_in_all, (1, 0), bf), None, None, None]
    x_up, x_down = after((x_up, x_down), parts[0])
    rows = 2 * half
    far = [send(x_up[:rows], Y_BY[3]), send(x_down[rows:], Y_BY[1])]
    parts[1], parts[3] = dot(x_up, w_in_all, (1, 0), bf), dot(x_down, w_in_all, (1, 0), bf)
    x_far = jnp.concatenate(after(far, parts[1], parts[3]))
    parts[2] = dot(x_far, w_in_all, (1, 0), bf)
    xs = [x_own, x_up, x_far, x_down]
    parts = jnp.stack([part.reshape(4, half, hidden) for part in parts], axis=1)

    c_up, c_down = after((c_up, c_down), parts)
    c_far = jnp.concatenate([send(c_up[:2], Z_BY[3]), send(c_down[2:], Z_BY[1])])
    cs = [c.reshape(-1, 2 * width) for c in (c_own, c_up, c_far, c_down)]

    pre = scatter_x(parts) + b_in[None, None, :]
    act, slope = gelu_pair(pre)
    act_all = gather_x(act.astype(bf))

    d_parts = jnp.stack([dot(c, w_out_all, (1, 1), bf).reshape(4, half, hidden) for c in cs])
    c_mine = jnp.concatenate([c[:, :width] for c in cs])
    c_other = jnp.concatenate([c[:, width:] for c in cs])
    act_all = after(act_all, c_mine, c_other, d_parts)
    d_act = swap_x(after(d_parts, act_all))

    act_all = act_all.reshape(-1, hidden)
    out_got = send(dot(act_all, c_other, (0, 0), bf), CORE)
    out_mine = (dot(act_all, c_mine, (0, 0)) + out_got.astype(f32)).astype(bf)
    out_deep = send(out_mine, DEPTH)
    d_w_out = out_mine.astype(f32) + out_deep.astype(f32)

    d_act = jnp.sum(after(d_act, out_mine).astype(f32), axis=0)
    d_pre_all = gather_x((d_act * slope).astype(bf))

    x_mine = jnp.concatenate([x[:, :width] for x in xs])
    x_other = jnp.concatenate([x[:, width:] for x in xs])
    x_other = jnp.concatenate([x_other, jnp.ones((x_other.shape[0], 16), bf)], axis=1)
    d_pre_all = after(d_pre_all, x_mine, x_other).swapaxes(0, 1)
    d_pre_rows = d_pre_all.reshape(-1, hidden)
    in_other = dot(x_other, after(d_pre_rows, out_deep), (0, 0), bf)
    in_got = send(in_other, CORE)
    d_pres = [d_pre_rows[4 * half * k : 4 * half * (k + 1)] for k in range(4)]
    d_pres = after(d_pres, in_other)
    shares = [dot(d_pres[k], w_in_all, (1, 1), bf) for k in (1, 3, 2)]
    got = [send(share, Y_BY[k]) for share, k in zip(shares, (1, 3, 2))]
    in_got = after(in_got, *shares)
    in_mine = (dot(x_mine, d_pre_rows, (0, 0)) + in_got[:width].astype(f32)).astype(bf)
    bias = (in_other[width:].astype(f32) + in_got[width:].astype(f32)).astype(bf)
    in_both = jnp.concatenate([in_mine, bias])
    in_deep = send(in_both, DEPTH)
    d_w_in = in_mine.astype(f32) + in_deep[:width].astype(f32)
    d_b_in = bias[0].astype(f32) + in_deep[width].astype(f32)

    total = dot(d_pres[0], w_in_all, (1, 1))
    for term in after(got, in_both):
        total = total + term.astype(f32)
    total = total.reshape(4, half, 2 * width)
    d_half = total[0]
    for j in range(1, 4):
        d_half = d_half + send(total[j].astype(bf), Z_BY[j]).astype(f32)
    d_half = d_half.astype(bf)
    mine, got = d_half[:, :width], send(d_half[:, width:], CORE)
    first = jnp.where(core == 0, mine, got)
    second = jnp.where(core == 0, got, mine)
    d_normed = jnp.concatenate([first, second], axis=0)
    return (d_normed, d_w_in, d_b_in, d_w_out)


def solution(mesh):
    placed = (
        P(("depth", "col"), "row"),
        P(("depth", "col")),
        P(("depth", "col"), "row"),
        P("row", "col"),
        P("col"),
        P("col", "row"),
    )
    return jax.shard_map(
        on_device,
        mesh=mesh,
        in_specs=placed,
        out_specs=(P(("depth", "col"), "row"), P("row", "col"), P("col"), P("col", "row")),
        check_vma=False,
    )
```

```python
import jax
import jax.numpy as jnp
from jax import lax
from jax.sharding import PartitionSpec as P

D = 6144
AXES = ("depth", "row", "col")

coeff = 0.7978845608028654


def sincos(positions, first, width):
    places = positions.astype(jnp.float32)[:, None]
    column = first + jnp.arange(width, dtype=jnp.int32)
    expo = (2 * (column // 2)).astype(jnp.float32) / jnp.float32(D)
    freq = jnp.power(jnp.float32(10000.0), -expo)
    angle = places * freq[None, :]
    return jnp.where((column % 2 == 0)[None, :], jnp.sin(angle), jnp.cos(angle))


def gelu_pair(value):
    inner = coeff * (value + 0.044715 * value * value * value)
    slope = jnp.tanh(inner)
    out = 0.5 * value * (1.0 + slope)
    grad = 0.5 * (1.0 + slope) + 0.5 * value * (1.0 - slope * slope) * coeff * (
        1.0 + 3.0 * 0.044715 * value * value
    )
    return (out, grad)


def moves(shift):
    def index(d, x, c, z, y):
        return ((d % 2) * 8 + (x % 4) * 2 + c % 2) * 16 + (z % 4) * 4 + y % 4

    return [
        (index(d, x, c, z, y), index(*shift(d, x, c, z, y)))
        for d in range(2)
        for x in range(4)
        for c in range(2)
        for z in range(4)
        for y in range(4)
    ]


CORE = moves(lambda d, x, c, z, y: (d, x, c + 1, z, y))
DEPTH = moves(lambda d, x, c, z, y: (d + 1, x, c, z, y))
Y_BY = [moves(lambda d, x, c, z, y, k=k: (d, x, c, z, y + k)) for k in range(4)]
Z_BY = [moves(lambda d, x, c, z, y, j=j: (d, x, c, z + j, y)) for j in range(4)]
X_SETS = [[c + 2 * x for x in range(4)] for c in range(2)]

Y_SETS = [[z * 4 + y for y in range(4)] for z in range(4)]


def send(value, pairs):
    return lax.ppermute(value, AXES, pairs)


def dot(a, b, contract, kind=jnp.float32):
    return lax.dot_general(
        a, b, ((contract[:1], contract[1:]), ((), ())), preferred_element_type=jnp.float32
    ).astype(kind)


def on_device(normed, positions, cotangent, w_in, b_in, w_out):
    bf, f32 = jnp.bfloat16, jnp.float32
    width = w_in.shape[0]
    hidden = w_in.shape[1]
    row = lax.axis_index("row")
    core = row % 2
    half = normed.shape[0] // 2

    def after(value, *others):
        return lax.optimization_barrier((value, *others))[0]

    def swap_x(value):
        return lax.all_to_all(value, "row", 0, 0, tiled=True, axis_index_groups=X_SETS)

    def scatter_x(part):
        return jnp.sum(swap_x(part).astype(f32), axis=0)

    def gather_x(own):
        return swap_x(jnp.broadcast_to(own[None], (4,) + own.shape))

    inputs = (normed.astype(f32) + sincos(positions, row * width, width)).astype(bf)
    both = jnp.stack([inputs, cotangent])
    mine = lax.dynamic_slice_in_dim(both, core * half, half, 1)
    other = send(lax.dynamic_slice_in_dim(both, (1 - core) * half, half, 1), CORE)
    x_half = jnp.concatenate([mine[0], other[0]], axis=1)
    c_half = jnp.concatenate([mine[1], other[1]], axis=1)
    w_in_got = send(w_in, CORE)
    w_out_got = send(w_out, CORE)
    w_in_all = jnp.concatenate([w_in, w_in_got], axis=0)
    w_out_all = jnp.concatenate([w_out, w_out_got], axis=1)

    x_one, x_three, x_two = (send(x_half, Z_BY[4 - j]) for j in (1, 3, 2))
    c_four = jnp.broadcast_to(after(c_half, x_half)[None], (4,) + c_half.shape)
    c_four = lax.all_to_all(c_four, "col", 0, 0, tiled=True, axis_index_groups=Y_SETS)
    y = lax.axis_index("col") % 4
    c_own = lax.dynamic_slice_in_dim(jnp.concatenate([c_four, c_four]), y, 4, 0)
    x_own = jnp.concatenate([x_half, x_one, x_two, x_three])

    x_up, x_down = send(x_own, Y_BY[3]), send(x_own, Y_BY[1])
    c_own = after(c_own, x_own, w_in_got, w_out_got)
    c_up, c_down = send(c_own, Z_BY[3]), send(c_own, Z_BY[1])
    parts = [dot(x_own, w_in_all, (1, 0), bf), None, None, None]
    x_up, x_down = after((x_up, x_down), parts[0])
    rows = 2 * half
    far = [send(x_up[:rows], Y_BY[3]), send(x_down[rows:], Y_BY[1])]
    parts[1], parts[3] = dot(x_up, w_in_all, (1, 0), bf), dot(x_down, w_in_all, (1, 0), bf)
    x_far = jnp.concatenate(after(far, parts[1], parts[3]))
    parts[2] = dot(x_far, w_in_all, (1, 0), bf)
    xs = [x_own, x_up, x_far, x_down]
    parts = [part.reshape(4, half, hidden) for part in parts]

    c_up, c_down = after((c_up, c_down), parts)
    c_far = jnp.concatenate([send(c_up[:2], Z_BY[3]), send(c_down[2:], Z_BY[1])])
    cs = [c.reshape(-1, 2 * width) for c in (c_own, c_up, c_far, c_down)]

    near = scatter_x(jnp.stack([parts[k] for k in (0, 1, 3)], axis=1))
    last = scatter_x(after(parts[2], near)[:, None])
    pre = jnp.concatenate([near[:2], last, near[2:]]) + b_in[None, None, :]
    act, slope = gelu_pair(pre)
    act_all = gather_x(act.astype(bf))

    d_parts = jnp.stack([dot(c, w_out_all, (1, 1), bf).reshape(4, half, hidden) for c in cs])
    d_parts, cs = after((d_parts, cs), act_all)
    d_act = swap_x(d_parts)
    c_mine = jnp.concatenate([c[:, :width] for c in cs])
    c_other = jnp.concatenate([c[:, width:] for c in cs])

    act_all = act_all.reshape(-1, hidden)
    cut = hidden // 2
    act_cuts = [act_all[:, :cut], act_all[:, cut:]]
    out_got = [send(dot(a, c_other, (0, 0), bf), CORE) for a in act_cuts]
    out_mine = [(dot(a, c_mine, (0, 0)) + got.astype(f32)).astype(bf) for a, got in zip(act_cuts, out_got)]
    out_deep = [send(mine, DEPTH) for mine in out_mine]
    d_w_out = jnp.concatenate([mine.astype(f32) + deep.astype(f32) for mine, deep in zip(out_mine, out_deep)])

    d_act = jnp.sum(d_act.astype(f32), axis=0)
    d_pre_all = gather_x((d_act * slope).astype(bf))

    cut = width // 2
    x_mine = [jnp.concatenate([x[:, i * cut : (i + 1) * cut] for x in xs]) for i in (0, 1)]
    x_other = [jnp.concatenate([x[:, i * cut : (i + 1) * cut] for x in xs]) for i in (2, 3)]
    x_other[1] = jnp.concatenate([x_other[1], jnp.ones((x_other[1].shape[0], 16), bf)], axis=1)
    d_pre_all = after(d_pre_all, x_mine, x_other).swapaxes(0, 1)
    d_pre_rows = d_pre_all.reshape(-1, hidden)
    in_other = [dot(x, after(d_pre_rows, out_deep), (0, 0), bf) for x in x_other]
    in_got = [send(other, CORE) for other in in_other]
    d_pres = [d_pre_rows[4 * half * k : 4 * half * (k + 1)] for k in range(4)]
    d_pres = after(d_pres, in_other)
    shares = [dot(d_pres[k], w_in_all, (1, 1), bf) for k in (1, 3, 2)]
    got = [send(share, Y_BY[k]) for share, k in zip(shares, (1, 3, 2))]
    in_got = after(in_got, *shares)
    in_mine = [(dot(x, d_pre_rows, (0, 0)) + got[:cut].astype(f32)).astype(bf) for x, got in zip(x_mine, in_got)]
    bias = (in_other[1][cut:].astype(f32) + in_got[1][cut:].astype(f32)).astype(bf)
    in_both = [in_mine[0], jnp.concatenate([in_mine[1], bias])]
    in_deep = [send(mine, DEPTH) for mine in in_both]
    d_w_in = jnp.concatenate([mine.astype(f32) + deep[:cut].astype(f32) for mine, deep in zip(in_mine, in_deep)])
    d_b_in = bias[0].astype(f32) + in_deep[1][cut].astype(f32)

    total = dot(d_pres[0], w_in_all, (1, 1))
    for term in after(got, in_both):
        total = total + term.astype(f32)
    total = total.reshape(4, half, 2 * width)
    d_half = total[0]
    for term in after([send(total[j].astype(bf), Z_BY[j]) for j in range(1, 4)], in_deep):
        d_half = d_half + term.astype(f32)
    d_half = d_half.astype(bf)
    mine, got = d_half[:, :width], send(d_half[:, width:], CORE)
    first = jnp.where(core == 0, mine, got)
    second = jnp.where(core == 0, got, mine)
    d_normed = jnp.concatenate([first, second], axis=0)
    return (d_normed, d_w_in, d_b_in, d_w_out)


def solution(mesh):
    placed = (
        P(("depth", "col"), "row"),
        P(("depth", "col")),
        P(("depth", "col"), "row"),
        P("row", "col"),
        P("col"),
        P("col", "row"),
    )
    return jax.shard_map(
        on_device,
        mesh=mesh,
        in_specs=placed,
        out_specs=(P(("depth", "col"), "row"), P("row", "col"), P("col"), P("col", "row")),
        check_vma=False,
    )
```

```python
import jax
import jax.numpy as jnp
from jax import lax
from jax.sharding import PartitionSpec as P

D = 6144
AXES = ("depth", "row", "col")

coeff = 0.7978845608028654


def sincos(positions, first, width):
    places = positions.astype(jnp.float32)[:, None]
    column = first + jnp.arange(width, dtype=jnp.int32)
    expo = (2 * (column // 2)).astype(jnp.float32) / jnp.float32(D)
    freq = jnp.power(jnp.float32(10000.0), -expo)
    angle = places * freq[None, :]
    return jnp.where((column % 2 == 0)[None, :], jnp.sin(angle), jnp.cos(angle))


def gelu_pair(value):
    inner = coeff * (value + 0.044715 * value * value * value)
    slope = jnp.tanh(inner)
    out = 0.5 * value * (1.0 + slope)
    grad = 0.5 * (1.0 + slope) + 0.5 * value * (1.0 - slope * slope) * coeff * (
        1.0 + 3.0 * 0.044715 * value * value
    )
    return (out, grad)


def moves(shift):
    def index(d, x, c, z, y):
        return ((d % 2) * 8 + (x % 4) * 2 + c % 2) * 16 + (z % 4) * 4 + y % 4

    return [
        (index(d, x, c, z, y), index(*shift(d, x, c, z, y)))
        for d in range(2)
        for x in range(4)
        for c in range(2)
        for z in range(4)
        for y in range(4)
    ]


CORE = moves(lambda d, x, c, z, y: (d, x, c + 1, z, y))
DEPTH = moves(lambda d, x, c, z, y: (d + 1, x, c, z, y))
Y_BY = [moves(lambda d, x, c, z, y, k=k: (d, x, c, z, y + k)) for k in range(4)]
Z_BY = [moves(lambda d, x, c, z, y, j=j: (d, x, c, z + j, y)) for j in range(4)]
X_SETS = [[c + 2 * x for x in range(4)] for c in range(2)]

Y_SETS = [[z * 4 + y for y in range(4)] for z in range(4)]


def send(value, pairs):
    return lax.ppermute(value, AXES, pairs)


def dot(a, b, contract, kind=jnp.float32):
    return lax.dot_general(
        a, b, ((contract[:1], contract[1:]), ((), ())), preferred_element_type=jnp.float32
    ).astype(kind)


def on_device(normed, positions, cotangent, w_in, b_in, w_out):
    bf, f32 = jnp.bfloat16, jnp.float32
    width = w_in.shape[0]
    hidden = w_in.shape[1]
    row = lax.axis_index("row")
    core = row % 2
    half = normed.shape[0] // 2

    def after(value, *others):
        return lax.optimization_barrier((value, *others))[0]

    def swap_x(value):
        return lax.all_to_all(value, "row", 0, 0, tiled=True, axis_index_groups=X_SETS)

    def scatter_x(part):
        return jnp.sum(swap_x(part).astype(f32), axis=0)

    def gather_x(own):
        return swap_x(jnp.broadcast_to(own[None], (4,) + own.shape))

    inputs = (normed.astype(f32) + sincos(positions, row * width, width)).astype(bf)
    both = jnp.stack([inputs, cotangent])
    mine = lax.dynamic_slice_in_dim(both, core * half, half, 1)
    other = send(lax.dynamic_slice_in_dim(both, (1 - core) * half, half, 1), CORE)
    x_half = jnp.concatenate([mine[0], other[0]], axis=1)
    c_half = jnp.concatenate([mine[1], other[1]], axis=1)
    w_in_got = send(w_in, CORE)
    w_out_got = send(w_out, CORE)
    w_in_all = jnp.concatenate([w_in, w_in_got], axis=0)
    w_out_all = jnp.concatenate([w_out, w_out_got], axis=1)

    x_one, x_three, x_two = (send(x_half, Z_BY[4 - j]) for j in (1, 3, 2))
    c_four = jnp.broadcast_to(after(c_half, x_half)[None], (4,) + c_half.shape)
    c_four = lax.all_to_all(c_four, "col", 0, 0, tiled=True, axis_index_groups=Y_SETS)
    y = lax.axis_index("col") % 4
    c_own = lax.dynamic_slice_in_dim(jnp.concatenate([c_four, c_four]), y, 4, 0)
    first = jnp.concatenate([x_half, x_one])
    x_two, x_three = after((x_two, x_three), first, w_in_all, w_out_all)
    up, down = send(first, Y_BY[3]), send(first, Y_BY[1])
    far = send(up, Y_BY[3])
    x_first = [first, up, far, down]
    second = jnp.concatenate([x_two, x_three])
    up, down = send(second, Y_BY[3]), send(second, Y_BY[1])
    far = send(down, Y_BY[1])
    x_second = [second, up, far, down]
    c_own = after(c_own, second)
    c_up, c_down = send(c_own, Z_BY[3]), send(c_own, Z_BY[1])
    xs = after([x for pair in zip(x_first, x_second) for x in pair], c_own)
    parts = [dot(x, w_in_all, (1, 0), bf).reshape(2, 1, half, hidden) for x in xs]
    parts = jnp.concatenate([jnp.concatenate(parts[i::2], axis=1) for i in (0, 1)])

    c_far = [send(c_up[:2], Z_BY[3]), send(c_down[2:], Z_BY[1])]

    pre = scatter_x(parts) + b_in[None, None, :]
    act, slope = gelu_pair(pre)
    act = act.astype(bf)
    act_all = gather_x(act)
    c_far = jnp.concatenate(after(c_far, act))
    cs = [c.reshape(-1, 2 * width) for c in (c_own, c_up, c_far, c_down)]

    d_parts = jnp.stack([dot(c, w_out_all, (1, 1), bf).reshape(4, half, hidden) for c in cs])
    d_parts, cs = after((d_parts, cs), act_all)
    d_act = swap_x(d_parts)
    c_mine = jnp.concatenate([c[:, :width] for c in cs])
    c_other = jnp.concatenate([c[:, width:] for c in cs])

    act_all = act_all.reshape(-1, hidden)
    cut = hidden // 2
    act_cuts = [act_all[:, :cut], act_all[:, cut:]]
    out_got = [send(dot(a, c_other, (0, 0), bf), CORE) for a in act_cuts]
    out_mine = [(dot(a, c_mine, (0, 0)) + got.astype(f32)).astype(bf) for a, got in zip(act_cuts, out_got)]
    out_deep = [send(mine, DEPTH) for mine in out_mine]

    d_act = jnp.sum(d_act.astype(f32), axis=0)
    d_pre_all = gather_x((d_act * slope).astype(bf))

    cut = width // 2
    x_mine = [jnp.concatenate([x[:, i * cut : (i + 1) * cut] for x in xs]) for i in (0, 1)]
    x_other = [jnp.concatenate([x[:, i * cut : (i + 1) * cut] for x in xs]) for i in (2, 3)]
    x_other[1] = jnp.concatenate([x_other[1], jnp.ones((x_other[1].shape[0], 16), bf)], axis=1)
    d_pre_all = after(d_pre_all, x_mine, x_other).swapaxes(0, 1)
    d_pre_rows = d_pre_all.reshape(-1, hidden)
    in_other = [dot(x, after(d_pre_rows, out_deep[0]), (0, 0), bf) for x in x_other]
    in_got = [send(other, CORE) for other in in_other]
    d_pres = [d_pre_rows[4 * half * k : 4 * half * (k + 1)] for k in range(4)]
    d_pres = after(d_pres, in_other)
    shares = [dot(d_pres[k], w_in_all, (1, 1), bf) for k in (1, 3, 2)]
    got = [send(share, Y_BY[k]) for share, k in zip(shares, (1, 3, 2))]
    out_deep = after(out_deep, shares)
    in_got = after(in_got, shares)
    d_w_out = jnp.concatenate([mine.astype(f32) + deep.astype(f32) for mine, deep in zip(out_mine, out_deep)])
    in_mine = [(dot(x, d_pre_rows, (0, 0)) + got[:cut].astype(f32)).astype(bf) for x, got in zip(x_mine, in_got)]
    bias = (in_other[1][cut:].astype(f32) + in_got[1][cut:].astype(f32)).astype(bf)
    in_both = [in_mine[0], jnp.concatenate([in_mine[1], bias])]
    in_deep = [send(mine, DEPTH) for mine in in_both]
    d_w_in = jnp.concatenate([mine.astype(f32) + deep[:cut].astype(f32) for mine, deep in zip(in_mine, in_deep)])
    d_b_in = bias[0].astype(f32) + in_deep[1][cut].astype(f32)

    total = dot(d_pres[0], w_in_all, (1, 1))
    for term in after(got, in_both):
        total = total + term.astype(f32)
    total = total.reshape(4, half, 2 * width)
    d_half = total[0]
    for term in after([send(total[j].astype(bf), Z_BY[j]) for j in range(1, 4)], in_deep):
        d_half = d_half + term.astype(f32)
    d_half = d_half.astype(bf)
    mine, got = d_half[:, :width], send(d_half[:, width:], CORE)
    first = jnp.where(core == 0, mine, got)
    second = jnp.where(core == 0, got, mine)
    d_normed = jnp.concatenate([first, second], axis=0)
    return (d_normed, d_w_in, d_b_in, d_w_out)


def solution(mesh):
    placed = (
        P(("depth", "col"), "row"),
        P(("depth", "col")),
        P(("depth", "col"), "row"),
        P("row", "col"),
        P("col"),
        P("col", "row"),
    )
    return jax.shard_map(
        on_device,
        mesh=mesh,
        in_specs=placed,
        out_specs=(P(("depth", "col"), "row"), P("row", "col"), P("col"), P("col", "row")),
        check_vma=False,
    )
```

```python
import jax
import jax.numpy as jnp
from jax import lax
from jax.sharding import PartitionSpec as P

D = 6144
AXES = ("depth", "row", "col")

coeff = 0.7978845608028654


def sincos(positions, first, width):
    places = positions.astype(jnp.float32)[:, None]
    column = first + jnp.arange(width, dtype=jnp.int32)
    expo = (2 * (column // 2)).astype(jnp.float32) / jnp.float32(D)
    freq = jnp.power(jnp.float32(10000.0), -expo)
    angle = places * freq[None, :]
    return jnp.where((column % 2 == 0)[None, :], jnp.sin(angle), jnp.cos(angle))


def gelu_pair(value):
    inner = coeff * (value + 0.044715 * value * value * value)
    slope = jnp.tanh(inner)
    out = 0.5 * value * (1.0 + slope)
    grad = 0.5 * (1.0 + slope) + 0.5 * value * (1.0 - slope * slope) * coeff * (
        1.0 + 3.0 * 0.044715 * value * value
    )
    return (out, grad)


def moves(shift):
    def index(d, x, c, z, y):
        return ((d % 2) * 8 + (x % 4) * 2 + c % 2) * 16 + (z % 4) * 4 + y % 4

    return [
        (index(d, x, c, z, y), index(*shift(d, x, c, z, y)))
        for d in range(2)
        for x in range(4)
        for c in range(2)
        for z in range(4)
        for y in range(4)
    ]


CORE = moves(lambda d, x, c, z, y: (d, x, c + 1, z, y))
DEPTH = moves(lambda d, x, c, z, y: (d + 1, x, c, z, y))
Y_BY = [moves(lambda d, x, c, z, y, k=k: (d, x, c, z, y + k)) for k in range(4)]
Z_BY = [moves(lambda d, x, c, z, y, j=j: (d, x, c, z + j, y)) for j in range(4)]
X_SETS = [[c + 2 * x for x in range(4)] for c in range(2)]

Y_SETS = [[z * 4 + y for y in range(4)] for z in range(4)]


def send(value, pairs):
    return lax.ppermute(value, AXES, pairs)


def dot(a, b, contract, kind=jnp.float32):
    return lax.dot_general(
        a, b, ((contract[:1], contract[1:]), ((), ())), preferred_element_type=jnp.float32
    ).astype(kind)


def on_device(normed, positions, cotangent, w_in, b_in, w_out):
    bf, f32 = jnp.bfloat16, jnp.float32
    width = w_in.shape[0]
    hidden = w_in.shape[1]
    row = lax.axis_index("row")
    core = row % 2
    half = normed.shape[0] // 2

    def after(value, *others):
        return lax.optimization_barrier((value, *others))[0]

    def swap_x(value):
        return lax.all_to_all(value, "row", 0, 0, tiled=True, axis_index_groups=X_SETS)

    def scatter_x(part):
        return jnp.sum(swap_x(part).astype(f32), axis=0)

    def gather_x(own):
        return swap_x(jnp.broadcast_to(own[None], (4,) + own.shape))

    inputs = (normed.astype(f32) + sincos(positions, row * width, width)).astype(bf)
    both = jnp.stack([inputs, cotangent])
    mine = lax.dynamic_slice_in_dim(both, core * half, half, 1)
    other = send(lax.dynamic_slice_in_dim(both, (1 - core) * half, half, 1), CORE)
    x_half = jnp.concatenate([mine[0], other[0]], axis=1)
    c_half = jnp.concatenate([mine[1], other[1]], axis=1)
    w_in_got = send(w_in, CORE)
    w_out_got = send(w_out, CORE)
    w_in_all = jnp.concatenate([w_in, w_in_got], axis=0)
    w_out_all = jnp.concatenate([w_out, w_out_got], axis=1)

    x_one, x_three, x_two = (send(x_half, Z_BY[4 - j]) for j in (1, 3, 2))
    c_four = jnp.broadcast_to(after(c_half, x_half)[None], (4,) + c_half.shape)
    c_four = lax.all_to_all(c_four, "col", 0, 0, tiled=True, axis_index_groups=Y_SETS)
    y = lax.axis_index("col") % 4
    c_own = lax.dynamic_slice_in_dim(jnp.concatenate([c_four, c_four]), y, 4, 0)
    x_own = jnp.concatenate([x_half, x_one, x_two, x_three])

    x_up, x_down = send(x_own, Y_BY[3]), send(x_own, Y_BY[1])
    c_own = after(c_own, x_own, w_in_got, w_out_got)
    c_up, c_down = send(c_own, Z_BY[3]), send(c_own, Z_BY[1])
    parts = [dot(x_own, w_in_all, (1, 0), bf), None, None, None]
    x_up, x_down = after((x_up, x_down), parts[0])
    rows = 2 * half
    far = [send(x_up[:rows], Y_BY[3]), send(x_down[rows:], Y_BY[1])]
    parts[1], parts[3] = dot(x_up, w_in_all, (1, 0), bf), dot(x_down, w_in_all, (1, 0), bf)
    x_far = jnp.concatenate(after(far, parts[1], parts[3]))
    parts[2] = dot(x_far, w_in_all, (1, 0), bf)
    xs = [x_own, x_up, x_far, x_down]
    parts = jnp.stack([part.reshape(4, half, hidden) for part in parts], axis=1)

    c_up, c_down = after((c_up, c_down), parts)
    c_far = jnp.concatenate([send(c_up[:2], Z_BY[3]), send(c_down[2:], Z_BY[1])])
    cs = [c.reshape(-1, 2 * width) for c in (c_own, c_up, c_far, c_down)]

    pre = scatter_x(parts) + b_in[None, None, :]
    act, slope = gelu_pair(pre)
    act_all = gather_x(act.astype(bf))

    d_parts = jnp.stack([dot(c, w_out_all, (1, 1), bf).reshape(4, half, hidden) for c in cs])
    c_mine = jnp.concatenate([c[:, :width] for c in cs])
    c_other = jnp.concatenate([c[:, width:] for c in cs])
    act_all = after(act_all, c_mine, c_other, d_parts)
    d_act = swap_x(after(d_parts, act_all))

    act_all = act_all.reshape(-1, hidden)
    cut = hidden // 2
    act_cuts = [act_all[:, :cut], act_all[:, cut:]]
    out_got = [send(dot(a, c_other, (0, 0), bf), CORE) for a in act_cuts]
    out_mine = [(dot(a, c_mine, (0, 0)) + got.astype(f32)).astype(bf) for a, got in zip(act_cuts, out_got)]
    out_deep = [send(mine, DEPTH) for mine in out_mine]

    d_act = jnp.sum(d_act.astype(f32), axis=0)
    d_pre_all = gather_x((d_act * slope).astype(bf))

    cut = width // 2
    x_mine = [jnp.concatenate([x[:, i * cut : (i + 1) * cut] for x in xs]) for i in (0, 1)]
    x_other = [jnp.concatenate([x[:, i * cut : (i + 1) * cut] for x in xs]) for i in (2, 3)]
    x_other[1] = jnp.concatenate([x_other[1], jnp.ones((x_other[1].shape[0], 16), bf)], axis=1)
    d_pre_all = after(d_pre_all, x_mine, x_other).swapaxes(0, 1)
    d_pre_rows = d_pre_all.reshape(-1, hidden)
    in_other = [dot(x, after(d_pre_rows, out_deep[0]), (0, 0), bf) for x in x_other]
    in_got = [send(other, CORE) for other in in_other]
    d_pres = [d_pre_rows[4 * half * k : 4 * half * (k + 1)] for k in range(4)]
    d_pres = after(d_pres, in_other)
    shares = [dot(d_pres[k], w_in_all, (1, 1), bf) for k in (1, 3, 2)]
    got = [send(share, Y_BY[k]) for share, k in zip(shares, (1, 3, 2))]
    out_deep = after(out_deep, shares)
    in_got = after(in_got, shares)
    d_w_out = jnp.concatenate([mine.astype(f32) + deep.astype(f32) for mine, deep in zip(out_mine, out_deep)])
    in_mine = [(dot(x, d_pre_rows, (0, 0)) + got[:cut].astype(f32)).astype(bf) for x, got in zip(x_mine, in_got)]
    bias = (in_other[1][cut:].astype(f32) + in_got[1][cut:].astype(f32)).astype(bf)
    in_both = [in_mine[0], jnp.concatenate([in_mine[1], bias])]
    in_deep = [send(mine, DEPTH) for mine in in_both]
    d_w_in = jnp.concatenate([mine.astype(f32) + deep[:cut].astype(f32) for mine, deep in zip(in_mine, in_deep)])
    d_b_in = bias[0].astype(f32) + in_deep[1][cut].astype(f32)

    total = dot(d_pres[0], w_in_all, (1, 1))
    for term in after(got, in_both):
        total = total + term.astype(f32)
    total = total.reshape(4, half, 2 * width)
    d_half = total[0]
    for term in after([send(total[j].astype(bf), Z_BY[j]) for j in range(1, 4)], in_deep):
        d_half = d_half + term.astype(f32)
    d_half = d_half.astype(bf)
    mine, got = d_half[:, :width], send(d_half[:, width:], CORE)
    first = jnp.where(core == 0, mine, got)
    second = jnp.where(core == 0, got, mine)
    d_normed = jnp.concatenate([first, second], axis=0)
    return (d_normed, d_w_in, d_b_in, d_w_out)


def solution(mesh):
    placed = (
        P(("depth", "col"), "row"),
        P(("depth", "col")),
        P(("depth", "col"), "row"),
        P("row", "col"),
        P("col"),
        P("col", "row"),
    )
    return jax.shard_map(
        on_device,
        mesh=mesh,
        in_specs=placed,
        out_specs=(P(("depth", "col"), "row"), P("row", "col"), P("col"), P("col", "row")),
        check_vma=False,
    )
```

```python
import jax
import jax.numpy as jnp
from jax import lax
from jax.sharding import PartitionSpec as P

D = 6144
AXES = ("depth", "row", "col")

coeff = 0.7978845608028654


def sincos(positions, first, width):
    places = positions.astype(jnp.float32)[:, None]
    column = first + jnp.arange(width, dtype=jnp.int32)
    expo = (2 * (column // 2)).astype(jnp.float32) / jnp.float32(D)
    freq = jnp.power(jnp.float32(10000.0), -expo)
    angle = places * freq[None, :]
    return jnp.where((column % 2 == 0)[None, :], jnp.sin(angle), jnp.cos(angle))


def gelu_pair(value):
    inner = coeff * (value + 0.044715 * value * value * value)
    slope = jnp.tanh(inner)
    out = 0.5 * value * (1.0 + slope)
    grad = 0.5 * (1.0 + slope) + 0.5 * value * (1.0 - slope * slope) * coeff * (
        1.0 + 3.0 * 0.044715 * value * value
    )
    return (out, grad)


def moves(shift):
    def index(d, x, c, z, y):
        return ((d % 2) * 8 + (x % 4) * 2 + c % 2) * 16 + (z % 4) * 4 + y % 4

    return [
        (index(d, x, c, z, y), index(*shift(d, x, c, z, y)))
        for d in range(2)
        for x in range(4)
        for c in range(2)
        for z in range(4)
        for y in range(4)
    ]


CORE = moves(lambda d, x, c, z, y: (d, x, c + 1, z, y))
DEPTH = moves(lambda d, x, c, z, y: (d + 1, x, c, z, y))
Y_BY = [moves(lambda d, x, c, z, y, k=k: (d, x, c, z, y + k)) for k in range(4)]
Z_BY = [moves(lambda d, x, c, z, y, j=j: (d, x, c, z + j, y)) for j in range(4)]
X_SETS = [[c + 2 * x for x in range(4)] for c in range(2)]

Y_SETS = [[z * 4 + y for y in range(4)] for z in range(4)]


def send(value, pairs):
    return lax.ppermute(value, AXES, pairs)


def dot(a, b, contract, kind=jnp.float32):
    return lax.dot_general(
        a, b, ((contract[:1], contract[1:]), ((), ())), preferred_element_type=jnp.float32
    ).astype(kind)


def on_device(normed, positions, cotangent, w_in, b_in, w_out):
    bf, f32 = jnp.bfloat16, jnp.float32
    width = w_in.shape[0]
    hidden = w_in.shape[1]
    row = lax.axis_index("row")
    core = row % 2
    half = normed.shape[0] // 2

    def after(value, *others):
        return lax.optimization_barrier((value, *others))[0]

    def swap_x(value):
        return lax.all_to_all(value, "row", 0, 0, tiled=True, axis_index_groups=X_SETS)

    def scatter_x(part):
        return jnp.sum(swap_x(part).astype(f32), axis=0)

    def gather_x(own):
        return swap_x(jnp.broadcast_to(own[None], (4,) + own.shape))

    inputs = (normed.astype(f32) + sincos(positions, row * width, width)).astype(bf)
    both = jnp.stack([inputs, cotangent])
    mine = lax.dynamic_slice_in_dim(both, core * half, half, 1)
    other = send(lax.dynamic_slice_in_dim(both, (1 - core) * half, half, 1), CORE)
    x_half = jnp.concatenate([mine[0], other[0]], axis=1)
    c_half = jnp.concatenate([mine[1], other[1]], axis=1)
    w_in_got = send(w_in, CORE)
    w_out_got = send(w_out, CORE)
    w_in_all = jnp.concatenate([w_in, w_in_got], axis=0)
    w_out_all = jnp.concatenate([w_out, w_out_got], axis=1)

    x_one, x_three, x_two = (send(x_half, Z_BY[4 - j]) for j in (1, 3, 2))
    c_four = jnp.broadcast_to(after(c_half, x_half)[None], (4,) + c_half.shape)
    c_four = lax.all_to_all(c_four, "col", 0, 0, tiled=True, axis_index_groups=Y_SETS)
    y = lax.axis_index("col") % 4
    c_own = lax.dynamic_slice_in_dim(jnp.concatenate([c_four, c_four]), y, 4, 0)
    x_own = jnp.concatenate([x_half, x_one, x_two, x_three])

    x_up, x_down = send(x_own, Y_BY[3]), send(x_own, Y_BY[1])
    c_own = after(c_own, x_own, w_in_got, w_out_got)
    c_up, c_down = send(c_own, Z_BY[3]), send(c_own, Z_BY[1])
    parts = [dot(x_own, w_in_all, (1, 0), bf), None, None, None]
    x_up, x_down = after((x_up, x_down), parts[0])
    rows = 2 * half
    far = [send(x_up[:rows], Y_BY[3]), send(x_down[rows:], Y_BY[1])]
    parts[1], parts[3] = dot(x_up, w_in_all, (1, 0), bf), dot(x_down, w_in_all, (1, 0), bf)
    x_far = jnp.concatenate(after(far, parts[1], parts[3]))
    parts[2] = dot(x_far, w_in_all, (1, 0), bf)
    xs = [x_own, x_up, x_far, x_down]
    parts = [part.reshape(4, half, hidden) for part in parts]

    c_up, c_down = after((c_up, c_down), parts)
    c_far = jnp.concatenate([send(c_up[:2], Z_BY[3]), send(c_down[2:], Z_BY[1])])
    cs = [c.reshape(-1, 2 * width) for c in (c_own, c_up, c_far, c_down)]

    near = scatter_x(jnp.stack([parts[k] for k in (0, 1, 3)], axis=1))
    last = scatter_x(after(parts[2], near)[:, None])
    pre = jnp.concatenate([near[:2], last, near[2:]]) + b_in[None, None, :]
    act, slope = gelu_pair(pre)
    act_all = gather_x(act.astype(bf))

    d_parts = jnp.stack([dot(c, w_out_all, (1, 1), bf).reshape(4, half, hidden) for c in cs])
    d_parts, cs = after((d_parts, cs), act_all)
    d_act = swap_x(d_parts)
    c_mine = jnp.concatenate([c[:, :width] for c in cs])
    c_other = jnp.concatenate([c[:, width:] for c in cs])

    act_all = act_all.reshape(-1, hidden)
    cut = hidden // 2
    act_cuts = [act_all[:, :cut], act_all[:, cut:]]
    out_got = [send(dot(a, c_other, (0, 0), bf), CORE) for a in act_cuts]
    out_mine = [(dot(a, c_mine, (0, 0)) + got.astype(f32)).astype(bf) for a, got in zip(act_cuts, out_got)]
    out_deep = [send(mine, DEPTH) for mine in out_mine]

    d_act = jnp.sum(d_act.astype(f32), axis=0)
    d_pre_all = gather_x((d_act * slope).astype(bf))

    cut = width // 2
    x_mine = [jnp.concatenate([x[:, i * cut : (i + 1) * cut] for x in xs]) for i in (0, 1)]
    x_other = [jnp.concatenate([x[:, i * cut : (i + 1) * cut] for x in xs]) for i in (2, 3)]
    x_other[1] = jnp.concatenate([x_other[1], jnp.ones((x_other[1].shape[0], 16), bf)], axis=1)
    d_pre_all = after(d_pre_all, x_mine, x_other).swapaxes(0, 1)
    d_pre_rows = d_pre_all.reshape(-1, hidden)
    in_other = [dot(x, after(d_pre_rows, out_mine), (0, 0), bf) for x in x_other]
    in_got = [send(other, CORE) for other in in_other]
    d_pres = [d_pre_rows[4 * half * k : 4 * half * (k + 1)] for k in range(4)]
    d_pres = after(d_pres, in_other)
    shares = [dot(d_pres[k], w_in_all, (1, 1), bf) for k in (2, 1, 3)]
    got = [send(share, Y_BY[k]) for share, k in zip(shares, (2, 1, 3))]
    in_got = after(in_got, *shares)
    out_deep = after(out_deep, *shares)
    d_w_out = jnp.concatenate([mine.astype(f32) + deep.astype(f32) for mine, deep in zip(out_mine, out_deep)])
    in_mine = [(dot(x, d_pre_rows, (0, 0)) + got[:cut].astype(f32)).astype(bf) for x, got in zip(x_mine, in_got)]
    bias = (in_other[1][cut:].astype(f32) + in_got[1][cut:].astype(f32)).astype(bf)
    in_both = [in_mine[0], jnp.concatenate([in_mine[1], bias])]
    in_deep = [send(mine, DEPTH) for mine in in_both]
    d_w_in = jnp.concatenate([mine.astype(f32) + deep[:cut].astype(f32) for mine, deep in zip(in_mine, in_deep)])

    total = dot(d_pres[0], w_in_all, (1, 1))
    for term in after(got, in_both):
        total = total + term.astype(f32)
    total = total.reshape(4, half, 2 * width)
    d_half = total[0]
    for term in after([send(total[j].astype(bf), Z_BY[j]) for j in range(1, 4)], in_deep):
        d_half = d_half + term.astype(f32)
    d_half = d_half.astype(bf)
    mine, got = d_half[:, :width], send(d_half[:, width:], CORE)
    first = jnp.where(core == 0, mine, got)
    second = jnp.where(core == 0, got, mine)
    d_normed = jnp.concatenate([first, second], axis=0)
    d_b_in = after(bias[0], d_normed, d_w_in, d_w_out).astype(f32) + in_deep[1][cut].astype(f32)
    return (d_normed, d_w_in, d_b_in, d_w_out)


def solution(mesh):
    placed = (
        P(("depth", "col"), "row"),
        P(("depth", "col")),
        P(("depth", "col"), "row"),
        P("row", "col"),
        P("col"),
        P("col", "row"),
    )
    return jax.shard_map(
        on_device,
        mesh=mesh,
        in_specs=placed,
        out_specs=(P(("depth", "col"), "row"), P("row", "col"), P("col"), P("col", "row")),
        check_vma=False,
    )
```

```python
import jax
import jax.numpy as jnp
from jax import lax
from jax.experimental import pallas as pl
from jax.sharding import PartitionSpec as P

D = 6144
AXES = ("depth", "row", "col")

coeff = 0.7978845608028654


def sincos(positions, first, width):
    places = positions.astype(jnp.float32)[:, None]
    column = first + jnp.arange(width, dtype=jnp.int32)
    expo = (2 * (column // 2)).astype(jnp.float32) / jnp.float32(D)
    freq = jnp.power(jnp.float32(10000.0), -expo)
    angle = places * freq[None, :]
    return jnp.where((column % 2 == 0)[None, :], jnp.sin(angle), jnp.cos(angle))


def gelu_pair(value):
    inner = coeff * (value + 0.044715 * value * value * value)
    slope = jnp.tanh(inner)
    out = 0.5 * value * (1.0 + slope)
    grad = 0.5 * (1.0 + slope) + 0.5 * value * (1.0 - slope * slope) * coeff * (
        1.0 + 3.0 * 0.044715 * value * value
    )
    return (out, grad)


def moves(shift):
    def index(d, x, c, z, y):
        return ((d % 2) * 8 + (x % 4) * 2 + c % 2) * 16 + (z % 4) * 4 + y % 4

    return [
        (index(d, x, c, z, y), index(*shift(d, x, c, z, y)))
        for d in range(2)
        for x in range(4)
        for c in range(2)
        for z in range(4)
        for y in range(4)
    ]


CORE = moves(lambda d, x, c, z, y: (d, x, c + 1, z, y))
DEPTH = moves(lambda d, x, c, z, y: (d + 1, x, c, z, y))
Y_BY = [moves(lambda d, x, c, z, y, k=k: (d, x, c, z, y + k)) for k in range(4)]
Z_BY = [moves(lambda d, x, c, z, y, j=j: (d, x, c, z + j, y)) for j in range(4)]
X_SETS = [[c + 2 * x for x in range(4)] for c in range(2)]

Y_SETS = [[z * 4 + y for y in range(4)] for z in range(4)]


def send(value, pairs):
    return lax.ppermute(value, AXES, pairs)


def dot(a, b, contract, kind=jnp.float32):
    return lax.dot_general(
        a, b, ((contract[:1], contract[1:]), ((), ())), preferred_element_type=jnp.float32
    ).astype(kind)


def share_kernel(d_ref, w_ref, *outs):
    for k, out in zip((2, 1, 3, 0), outs):
        rows = d_ref[:, k].reshape(out.shape[0], d_ref.shape[3])
        out[...] = lax.dot_general(
            rows, w_ref[...], (((1,), (1,)), ((), ())), preferred_element_type=jnp.float32
        ).astype(out.dtype)


def all_shares(d_pre, w):
    rows, wide, hidden = 4 * d_pre.shape[2], w.shape[0], w.shape[1]
    tile = 256
    return pl.pallas_call(
        share_kernel,
        grid=(wide // tile,),
        in_specs=[
            pl.BlockSpec(d_pre.shape, lambda n: (0, 0, 0, 0)),
            pl.BlockSpec((tile, hidden), lambda n: (n, 0)),
        ],
        out_specs=[pl.BlockSpec((rows, tile), lambda n: (0, n))] * 4,
        out_shape=[jax.ShapeDtypeStruct((rows, wide), kind) for kind in [d_pre.dtype] * 3 + [jnp.float32]],
        cost_estimate=pl.CostEstimate(
            flops=8 * rows * wide * hidden, bytes_accessed=2 * (d_pre.size + w.size + 5 * rows * wide), transcendentals=0
        ),
    )(d_pre, w)


def columns_kernel(a_ref, b_ref, *refs):
    product = lax.dot_general(
        a_ref[...], b_ref[...], (((0,), (0,)), ((), ())), preferred_element_type=jnp.float32
    )
    for got_ref in refs[:-1]:
        product = product + got_ref[...].astype(jnp.float32)
    refs[-1][...] = product.astype(refs[-1].dtype)


def columns_by(a, b, *got):
    tile = 128
    rows, size = a.shape[1], b.shape[1]
    return pl.pallas_call(
        columns_kernel,
        grid=(rows // tile,),
        in_specs=[
            pl.BlockSpec((a.shape[0], tile), lambda n: (0, n)),
            pl.BlockSpec(b.shape, lambda n: (0, 0)),
            *[pl.BlockSpec((tile, size), lambda n: (n, 0))] * len(got),
        ],
        out_specs=pl.BlockSpec((tile, size), lambda n: (n, 0)),
        out_shape=jax.ShapeDtypeStruct((rows, size), a.dtype),
        cost_estimate=pl.CostEstimate(
            flops=2 * a.size * size, bytes_accessed=2 * (a.size + b.size + 2 * rows * size), transcendentals=0
        ),
    )(a, b, *got)


def on_device(normed, positions, cotangent, w_in, b_in, w_out):
    bf, f32 = jnp.bfloat16, jnp.float32
    width = w_in.shape[0]
    hidden = w_in.shape[1]
    row = lax.axis_index("row")
    core = row % 2
    half = normed.shape[0] // 2

    def after(value, *others):
        return lax.optimization_barrier((value, *others))[0]

    def swap_x(value):
        return lax.all_to_all(value, "row", 0, 0, tiled=True, axis_index_groups=X_SETS)

    def scatter_x(part):
        return jnp.sum(swap_x(part).astype(f32), axis=0)

    def gather_x(own):
        return swap_x(jnp.broadcast_to(own[None], (4,) + own.shape))

    inputs = (normed.astype(f32) + sincos(positions, row * width, width)).astype(bf)
    both = jnp.stack([inputs, cotangent])
    mine = lax.dynamic_slice_in_dim(both, core * half, half, 1)
    other = send(lax.dynamic_slice_in_dim(both, (1 - core) * half, half, 1), CORE)
    x_half = jnp.concatenate([mine[0], other[0]], axis=1)
    c_half = jnp.concatenate([mine[1], other[1]], axis=1)
    w_in_got = send(w_in, CORE)
    w_out_got = send(w_out, CORE)
    w_in_all = jnp.concatenate([w_in, w_in_got], axis=0)
    w_out_all = jnp.concatenate([w_out, w_out_got], axis=1)

    x_one, x_three, x_two = (send(x_half, Z_BY[4 - j]) for j in (1, 3, 2))
    c_four = jnp.broadcast_to(after(c_half, x_half)[None], (4,) + c_half.shape)
    c_four = lax.all_to_all(c_four, "col", 0, 0, tiled=True, axis_index_groups=Y_SETS)
    y = lax.axis_index("col") % 4
    c_own = lax.dynamic_slice_in_dim(jnp.concatenate([c_four, c_four]), y, 4, 0)
    x_own = jnp.concatenate([x_half, x_one, x_two, x_three])

    x_up, x_down = send(x_own, Y_BY[3]), send(x_own, Y_BY[1])
    c_own = after(c_own, x_own, w_in_got, w_out_got)
    c_up, c_down = send(c_own, Z_BY[3]), send(c_own, Z_BY[1])
    parts = [dot(x_own, w_in_all, (1, 0), bf), None, None, None]
    x_up, x_down = after((x_up, x_down), parts[0])
    rows = 2 * half
    far = [send(x_up[:rows], Y_BY[3]), send(x_down[rows:], Y_BY[1])]
    parts[1], parts[3] = dot(x_up, w_in_all, (1, 0), bf), dot(x_down, w_in_all, (1, 0), bf)
    x_far = jnp.concatenate(after(far, parts[1], parts[3]))
    parts[2] = dot(x_far, w_in_all, (1, 0), bf)
    xs = [x_own, x_up, x_far, x_down]
    parts = [part.reshape(4, half, hidden) for part in parts]

    c_up, c_down = after((c_up, c_down), parts)
    c_far = jnp.concatenate([send(c_up[:2], Z_BY[3]), send(c_down[2:], Z_BY[1])])
    cs = [c.reshape(-1, 2 * width) for c in (c_own, c_up, c_far, c_down)]

    near = scatter_x(jnp.stack([parts[k] for k in (0, 1, 3)], axis=1))
    last = scatter_x(after(parts[2], near)[:, None])
    pre = jnp.concatenate([near[:2], last, near[2:]]) + b_in[None, None, :]
    act, slope = gelu_pair(pre)
    act_all = gather_x(act.astype(bf))

    d_parts = jnp.stack([dot(c, w_out_all, (1, 1), bf).reshape(4, half, hidden) for c in cs])
    d_parts, cs = after((d_parts, cs), act_all)
    d_act = swap_x(d_parts)
    c_mine = jnp.concatenate([c[:, :width] for c in cs])
    c_other = jnp.concatenate([c[:, width:] for c in cs])

    act_all = act_all.reshape(-1, hidden)
    cut = hidden // 2
    act_cuts = [act_all[:, :cut], act_all[:, cut:]]
    out_got = [send(dot(a, c_other, (0, 0), bf), CORE) for a in act_cuts]
    out_mine = [(dot(a, c_mine, (0, 0)) + got.astype(f32)).astype(bf) for a, got in zip(act_cuts, out_got)]
    out_deep = [send(mine, DEPTH) for mine in out_mine]

    d_act = jnp.sum(d_act.astype(f32), axis=0)
    d_pre_all = gather_x((d_act * slope).astype(bf))

    cut = width // 2
    x_mine = [jnp.concatenate([x[:, i * cut : (i + 1) * cut] for x in xs]) for i in (0, 1)]
    x_other = [jnp.concatenate([x[:, i * cut : (i + 1) * cut] for x in xs]) for i in (2, 3)]
    x_other[1] = jnp.concatenate([x_other[1], jnp.ones((x_other[1].shape[0], 16), bf)], axis=1)
    d_raw = after(d_pre_all, x_mine, x_other)
    d_pre_all = d_raw.swapaxes(0, 1)
    d_pre_rows = d_pre_all.reshape(-1, hidden)
    d_pre_rows = after(d_pre_rows, out_mine)
    in_other = [columns_by(x_other[0], d_pre_rows), dot(x_other[1], d_pre_rows, (0, 0), bf)]
    in_got = [send(other, CORE) for other in in_other]
    *shares, total = all_shares(after(d_raw, in_other), w_in_all)
    got = [send(share, Y_BY[k]) for share, k in zip(shares, (2, 1, 3))]
    in_got = after(in_got, *shares)
    out_deep = after(out_deep, *shares)
    d_w_out = jnp.concatenate([mine.astype(f32) + deep.astype(f32) for mine, deep in zip(out_mine, out_deep)])
    in_mine = [columns_by(x, d_pre_rows, got) for x, got in zip(x_mine, in_got)]
    bias = (in_other[1][cut:].astype(f32) + in_got[1][cut:].astype(f32)).astype(bf)
    in_both = [in_mine[0], jnp.concatenate([in_mine[1], bias])]
    in_deep = [send(mine, DEPTH) for mine in in_both]
    d_w_in = jnp.concatenate([mine.astype(f32) + deep[:cut].astype(f32) for mine, deep in zip(in_mine, in_deep)])

    for term in after(got, in_both):
        total = total + term.astype(f32)
    total = total.reshape(4, half, 2 * width)
    d_half = total[0]
    for term in after([send(total[j].astype(bf), Z_BY[j]) for j in range(1, 4)], in_deep):
        d_half = d_half + term.astype(f32)
    d_half = d_half.astype(bf)
    mine, got = d_half[:, :width], send(d_half[:, width:], CORE)
    first = jnp.where(core == 0, mine, got)
    second = jnp.where(core == 0, got, mine)
    d_normed = jnp.concatenate([first, second], axis=0)
    d_b_in = after(bias[0], d_normed, d_w_in, d_w_out).astype(f32) + in_deep[1][cut].astype(f32)
    return (d_normed, d_w_in, d_b_in, d_w_out)


def solution(mesh):
    placed = (
        P(("depth", "col"), "row"),
        P(("depth", "col")),
        P(("depth", "col"), "row"),
        P("row", "col"),
        P("col"),
        P("col", "row"),
    )
    return jax.shard_map(
        on_device,
        mesh=mesh,
        in_specs=placed,
        out_specs=(P(("depth", "col"), "row"), P("row", "col"), P("col"), P("col", "row")),
        check_vma=False,
    )
```

```python
import jax
import jax.numpy as jnp
from jax import lax
from jax.experimental import pallas as pl
from jax.sharding import PartitionSpec as P

D = 6144
AXES = ("depth", "row", "col")

coeff = 0.7978845608028654


def add_table_kernel(place_ref, freq_ref, normed_ref, out_ref):
    angle = place_ref[...] * freq_ref[...]
    even = lax.broadcasted_iota(jnp.int32, angle.shape, 1) % 2 == 0
    table = jnp.where(even, jnp.sin(angle), jnp.cos(angle))
    out_ref[...] = (normed_ref[...].astype(jnp.float32) + table).astype(out_ref.dtype)


def add_table(normed, positions, first):
    rows, width = normed.shape
    column = first + jnp.arange(width, dtype=jnp.int32)
    expo = (2 * (column // 2)).astype(jnp.float32) / jnp.float32(D)
    freq = jnp.power(jnp.float32(10000.0), -expo)
    tile = 16
    return pl.pallas_call(
        add_table_kernel,
        grid=(rows // tile,),
        in_specs=[
            pl.BlockSpec((tile, 1), lambda n: (n, 0)),
            pl.BlockSpec((1, width), lambda n: (0, 0)),
            pl.BlockSpec((tile, width), lambda n: (n, 0)),
        ],
        out_specs=pl.BlockSpec((tile, width), lambda n: (n, 0)),
        out_shape=jax.ShapeDtypeStruct(normed.shape, normed.dtype),
    )(positions.astype(jnp.float32)[:, None], freq[None, :], normed)


def gelu_pair(value):
    inner = coeff * (value + 0.044715 * value * value * value)
    slope = jnp.tanh(inner)
    out = 0.5 * value * (1.0 + slope)
    grad = 0.5 * (1.0 + slope) + 0.5 * value * (1.0 - slope * slope) * coeff * (
        1.0 + 3.0 * 0.044715 * value * value
    )
    return (out, grad)


def moves(shift):
    def index(d, x, c, z, y):
        return ((d % 2) * 8 + (x % 4) * 2 + c % 2) * 16 + (z % 4) * 4 + y % 4

    return [
        (index(d, x, c, z, y), index(*shift(d, x, c, z, y)))
        for d in range(2)
        for x in range(4)
        for c in range(2)
        for z in range(4)
        for y in range(4)
    ]


CORE = moves(lambda d, x, c, z, y: (d, x, c + 1, z, y))
DEPTH = moves(lambda d, x, c, z, y: (d + 1, x, c, z, y))
Y_BY = [moves(lambda d, x, c, z, y, k=k: (d, x, c, z, y + k)) for k in range(4)]
Z_BY = [moves(lambda d, x, c, z, y, j=j: (d, x, c, z + j, y)) for j in range(4)]
X_SETS = [[c + 2 * x for x in range(4)] for c in range(2)]

Y_SETS = [[z * 4 + y for y in range(4)] for z in range(4)]


def send(value, pairs):
    return lax.ppermute(value, AXES, pairs)


def dot(a, b, contract, kind=jnp.float32):
    return lax.dot_general(
        a, b, ((contract[:1], contract[1:]), ((), ())), preferred_element_type=jnp.float32
    ).astype(kind)


def share_kernel(d_ref, w_ref, *outs):
    for k, out in zip((2, 1, 3, 0), outs):
        rows = d_ref[:, k].reshape(out.shape[0], d_ref.shape[3])
        out[...] = lax.dot_general(
            rows, w_ref[...], (((1,), (1,)), ((), ())), preferred_element_type=jnp.float32
        ).astype(out.dtype)


def all_shares(d_pre, w):
    rows, wide, hidden = 4 * d_pre.shape[2], w.shape[0], w.shape[1]
    tile = 256
    return pl.pallas_call(
        share_kernel,
        grid=(wide // tile,),
        in_specs=[
            pl.BlockSpec(d_pre.shape, lambda n: (0, 0, 0, 0)),
            pl.BlockSpec((tile, hidden), lambda n: (n, 0)),
        ],
        out_specs=[pl.BlockSpec((rows, tile), lambda n: (0, n))] * 4,
        out_shape=[jax.ShapeDtypeStruct((rows, wide), kind) for kind in [d_pre.dtype] * 3 + [jnp.float32]],
        cost_estimate=pl.CostEstimate(
            flops=8 * rows * wide * hidden, bytes_accessed=2 * (d_pre.size + w.size + 5 * rows * wide), transcendentals=0
        ),
    )(d_pre, w)


def on_device(normed, positions, cotangent, w_in, b_in, w_out):
    bf, f32 = jnp.bfloat16, jnp.float32
    width = w_in.shape[0]
    hidden = w_in.shape[1]
    row = lax.axis_index("row")
    core = row % 2
    half = normed.shape[0] // 2

    def after(value, *others):
        return lax.optimization_barrier((value, *others))[0]

    def swap_x(value):
        return lax.all_to_all(value, "row", 0, 0, tiled=True, axis_index_groups=X_SETS)

    def scatter_x(part):
        return jnp.sum(swap_x(part).astype(f32), axis=0)

    def gather_x(own):
        return swap_x(jnp.broadcast_to(own[None], (4,) + own.shape))

    inputs = add_table(normed, positions, row * width)
    both = jnp.stack([inputs, cotangent])
    mine = lax.dynamic_slice_in_dim(both, core * half, half, 1)
    other = send(lax.dynamic_slice_in_dim(both, (1 - core) * half, half, 1), CORE)
    x_half = jnp.concatenate([mine[0], other[0]], axis=1)
    c_half = jnp.concatenate([mine[1], other[1]], axis=1)
    w_in_got = send(w_in, CORE)
    w_out_got = send(w_out, CORE)
    w_in_all = jnp.concatenate([w_in, w_in_got], axis=0)
    w_out_all = jnp.concatenate([w_out, w_out_got], axis=1)

    x_one, x_three, x_two = (send(x_half, Z_BY[4 - j]) for j in (1, 3, 2))
    c_four = jnp.broadcast_to(after(c_half, x_half)[None], (4,) + c_half.shape)
    c_four = lax.all_to_all(c_four, "col", 0, 0, tiled=True, axis_index_groups=Y_SETS)
    y = lax.axis_index("col") % 4
    c_own = lax.dynamic_slice_in_dim(jnp.concatenate([c_four, c_four]), y, 4, 0)
    x_own = jnp.concatenate([x_half, x_one, x_two, x_three])

    x_up, x_down = send(x_own, Y_BY[3]), send(x_own, Y_BY[1])
    c_own = after(c_own, x_own, w_in_got, w_out_got)
    c_up, c_down = send(c_own, Z_BY[3]), send(c_own, Z_BY[1])
    parts = [dot(x_own, w_in_all, (1, 0), bf), None, None, None]
    x_up, x_down = after((x_up, x_down), parts[0])
    rows = 2 * half
    far = [send(x_up[:rows], Y_BY[3]), send(x_down[rows:], Y_BY[1])]
    parts[1], parts[3] = dot(x_up, w_in_all, (1, 0), bf), dot(x_down, w_in_all, (1, 0), bf)
    x_far = jnp.concatenate(after(far, parts[1], parts[3]))
    parts[2] = dot(x_far, w_in_all, (1, 0), bf)
    xs = [x_own, x_up, x_far, x_down]
    parts = [part.reshape(4, half, hidden) for part in parts]

    c_up, c_down = after((c_up, c_down), parts)
    c_far = jnp.concatenate([send(c_up[:2], Z_BY[3]), send(c_down[2:], Z_BY[1])])
    cs = [c.reshape(-1, 2 * width) for c in (c_own, c_up, c_far, c_down)]

    near = scatter_x(jnp.stack([parts[k] for k in (0, 1, 3)], axis=1))
    last = scatter_x(after(parts[2], near)[:, None])
    pre = jnp.concatenate([near[:2], last, near[2:]]) + b_in[None, None, :]
    act, slope = gelu_pair(pre)
    act_all = gather_x(act.astype(bf))

    d_parts = jnp.stack([dot(c, w_out_all, (1, 1), bf).reshape(4, half, hidden) for c in cs])
    d_parts, cs = after((d_parts, cs), act_all)
    d_act = swap_x(d_parts)
    c_mine = jnp.concatenate([c[:, :width] for c in cs])
    c_other = jnp.concatenate([c[:, width:] for c in cs])

    act_all = act_all.reshape(-1, hidden)
    cut = hidden // 2
    act_cuts = [act_all[:, :cut], act_all[:, cut:]]
    out_got = [send(dot(a, c_other, (0, 0), bf), CORE) for a in act_cuts]
    out_mine = [(dot(a, c_mine, (0, 0)) + got.astype(f32)).astype(bf) for a, got in zip(act_cuts, out_got)]
    out_deep = [send(mine, DEPTH) for mine in out_mine]

    d_act = jnp.sum(d_act.astype(f32), axis=0)
    d_pre_all = gather_x((d_act * slope).astype(bf))

    cut = width // 2
    x_mine = [jnp.concatenate([x[:, i * cut : (i + 1) * cut] for x in xs]) for i in (0, 1)]
    x_other = [jnp.concatenate([x[:, i * cut : (i + 1) * cut] for x in xs]) for i in (2, 3)]
    x_other[1] = jnp.concatenate([x_other[1], jnp.ones((x_other[1].shape[0], 16), bf)], axis=1)
    d_raw = after(d_pre_all, x_mine, x_other)
    d_pre_all = d_raw.swapaxes(0, 1)
    d_pre_rows = d_pre_all.reshape(-1, hidden)
    in_other = [dot(x, after(d_pre_rows, out_mine), (0, 0), bf) for x in x_other]
    in_got = [send(other, CORE) for other in in_other]
    *shares, total = all_shares(after(d_raw, in_other), w_in_all)
    got = [send(share, Y_BY[k]) for share, k in zip(shares, (2, 1, 3))]
    in_got = after(in_got, *shares)
    out_deep = after(out_deep, *shares)
    d_w_out = jnp.concatenate(out_mine).astype(f32) + jnp.concatenate(out_deep).astype(f32)
    in_mine = [(dot(x, d_pre_rows, (0, 0)) + got[:cut].astype(f32)).astype(bf) for x, got in zip(x_mine, in_got)]
    bias = (in_other[1][cut:].astype(f32) + in_got[1][cut:].astype(f32)).astype(bf)
    in_both = [in_mine[0], jnp.concatenate([in_mine[1], bias])]
    in_deep = [send(mine, DEPTH) for mine in in_both]
    d_w_in = jnp.concatenate(in_mine).astype(f32) + jnp.concatenate([deep[:cut] for deep in in_deep]).astype(f32)

    for term in after(got, in_both):
        total = total + term.astype(f32)
    total = total.reshape(4, half, 2 * width)
    d_half = total[0]
    for term in after([send(total[j].astype(bf), Z_BY[j]) for j in range(1, 4)], in_deep):
        d_half = d_half + term.astype(f32)
    d_half = d_half.astype(bf)
    mine, got = d_half[:, :width], send(d_half[:, width:], CORE)
    first = jnp.where(core == 0, mine, got)
    second = jnp.where(core == 0, got, mine)
    d_normed = jnp.concatenate([first, second], axis=0)
    d_b_in = after(bias[0], d_normed, d_w_in, d_w_out).astype(f32) + in_deep[1][cut].astype(f32)
    return (d_normed, d_w_in, d_b_in, d_w_out)


def solution(mesh):
    placed = (
        P(("depth", "col"), "row"),
        P(("depth", "col")),
        P(("depth", "col"), "row"),
        P("row", "col"),
        P("col"),
        P("col", "row"),
    )
    return jax.shard_map(
        on_device,
        mesh=mesh,
        in_specs=placed,
        out_specs=(P(("depth", "col"), "row"), P("row", "col"), P("col"), P("col", "row")),
        check_vma=False,
    )
```

```python
import jax
import jax.numpy as jnp
from jax import lax
from jax.experimental import pallas as pl
from jax.sharding import PartitionSpec as P

D = 6144
AXES = ("depth", "row", "col")

coeff = 0.7978845608028654


def add_table_kernel(place_ref, freq_ref, normed_ref, out_ref):
    angle = place_ref[...] * freq_ref[...]
    even = lax.broadcasted_iota(jnp.int32, angle.shape, 1) % 2 == 0
    table = jnp.where(even, jnp.sin(angle), jnp.cos(angle))
    out_ref[...] = (normed_ref[...].astype(jnp.float32) + table).astype(out_ref.dtype)


def add_table(normed, positions, first):
    rows, width = normed.shape
    column = first + jnp.arange(width, dtype=jnp.int32)
    expo = (2 * (column // 2)).astype(jnp.float32) / jnp.float32(D)
    freq = jnp.power(jnp.float32(10000.0), -expo)
    tile = 16
    return pl.pallas_call(
        add_table_kernel,
        grid=(rows // tile,),
        in_specs=[
            pl.BlockSpec((tile, 1), lambda n: (n, 0)),
            pl.BlockSpec((1, width), lambda n: (0, 0)),
            pl.BlockSpec((tile, width), lambda n: (n, 0)),
        ],
        out_specs=pl.BlockSpec((tile, width), lambda n: (n, 0)),
        out_shape=jax.ShapeDtypeStruct(normed.shape, normed.dtype),
    )(positions.astype(jnp.float32)[:, None], freq[None, :], normed)


def gelu_pair(value):
    inner = coeff * (value + 0.044715 * value * value * value)
    slope = jnp.tanh(inner)
    out = 0.5 * value * (1.0 + slope)
    grad = 0.5 * (1.0 + slope) + 0.5 * value * (1.0 - slope * slope) * coeff * (
        1.0 + 3.0 * 0.044715 * value * value
    )
    return (out, grad)


def moves(shift):
    def index(d, x, c, z, y):
        return ((d % 2) * 8 + (x % 4) * 2 + c % 2) * 16 + (z % 4) * 4 + y % 4

    return [
        (index(d, x, c, z, y), index(*shift(d, x, c, z, y)))
        for d in range(2)
        for x in range(4)
        for c in range(2)
        for z in range(4)
        for y in range(4)
    ]


CORE = moves(lambda d, x, c, z, y: (d, x, c + 1, z, y))
DEPTH = moves(lambda d, x, c, z, y: (d + 1, x, c, z, y))
Y_BY = [moves(lambda d, x, c, z, y, k=k: (d, x, c, z, y + k)) for k in range(4)]
Z_BY = [moves(lambda d, x, c, z, y, j=j: (d, x, c, z + j, y)) for j in range(4)]
X_SETS = [[c + 2 * x for x in range(4)] for c in range(2)]

Y_SETS = [[z * 4 + y for y in range(4)] for z in range(4)]


def send(value, pairs):
    return lax.ppermute(value, AXES, pairs)


def dot(a, b, contract, kind=jnp.float32):
    return lax.dot_general(
        a, b, ((contract[:1], contract[1:]), ((), ())), preferred_element_type=jnp.float32
    ).astype(kind)


def share_kernel(d_ref, w_ref, *outs):
    for k, out in zip((1, 3, 0), outs):
        rows = d_ref[:, k].reshape(out.shape[0], d_ref.shape[3])
        out[...] = lax.dot_general(
            rows, w_ref[...], (((1,), (1,)), ((), ())), preferred_element_type=jnp.float32
        ).astype(out.dtype)


def near_shares(d_pre, w):
    rows, wide, hidden = 4 * d_pre.shape[2], w.shape[0], w.shape[1]
    tile = 256
    return pl.pallas_call(
        share_kernel,
        grid=(wide // tile,),
        in_specs=[
            pl.BlockSpec(d_pre.shape, lambda n: (0, 0, 0, 0)),
            pl.BlockSpec((tile, hidden), lambda n: (n, 0)),
        ],
        out_specs=[pl.BlockSpec((rows, tile), lambda n: (0, n))] * 3,
        out_shape=[jax.ShapeDtypeStruct((rows, wide), kind) for kind in [d_pre.dtype] * 2 + [jnp.float32]],
        cost_estimate=pl.CostEstimate(
            flops=6 * rows * wide * hidden, bytes_accessed=2 * (d_pre.size + w.size + 4 * rows * wide), transcendentals=0
        ),
    )(d_pre, w)


def on_device(normed, positions, cotangent, w_in, b_in, w_out):
    bf, f32 = jnp.bfloat16, jnp.float32
    width = w_in.shape[0]
    hidden = w_in.shape[1]
    row = lax.axis_index("row")
    core = row % 2
    half = normed.shape[0] // 2

    def after(value, *others):
        return lax.optimization_barrier((value, *others))[0]

    def swap_x(value):
        return lax.all_to_all(value, "row", 0, 0, tiled=True, axis_index_groups=X_SETS)

    def scatter_x(part):
        return jnp.sum(swap_x(part).astype(f32), axis=0)

    def gather_x(own):
        return swap_x(jnp.broadcast_to(own[None], (4,) + own.shape))

    inputs = add_table(normed, positions, row * width)
    both = jnp.stack([inputs, cotangent])
    mine = lax.dynamic_slice_in_dim(both, core * half, half, 1)
    other = send(lax.dynamic_slice_in_dim(both, (1 - core) * half, half, 1), CORE)
    x_half = jnp.concatenate([mine[0], other[0]], axis=1)
    c_half = jnp.concatenate([mine[1], other[1]], axis=1)
    w_in_got = send(w_in, CORE)
    w_out_got = send(w_out, CORE)
    w_in_all = jnp.concatenate([w_in, w_in_got], axis=0)
    w_out_all = jnp.concatenate([w_out, w_out_got], axis=1)

    x_one, x_three, x_two = (send(x_half, Z_BY[4 - j]) for j in (1, 3, 2))
    c_four = jnp.broadcast_to(after(c_half, x_half)[None], (4,) + c_half.shape)
    c_four = lax.all_to_all(c_four, "col", 0, 0, tiled=True, axis_index_groups=Y_SETS)
    y = lax.axis_index("col") % 4
    c_own = lax.dynamic_slice_in_dim(jnp.concatenate([c_four, c_four]), y, 4, 0)
    x_own = jnp.concatenate([x_half, x_one, x_two, x_three])

    x_up, x_down = send(x_own, Y_BY[3]), send(x_own, Y_BY[1])
    c_own = after(c_own, x_own, w_in_got, w_out_got)
    c_up, c_down = send(c_own, Z_BY[3]), send(c_own, Z_BY[1])
    parts = [dot(x_own, w_in_all, (1, 0), bf), None, None, None]
    x_up, x_down = after((x_up, x_down), parts[0])
    rows = 2 * half
    far = [send(x_up[:rows], Y_BY[3]), send(x_down[rows:], Y_BY[1])]
    parts[1], parts[3] = dot(x_up, w_in_all, (1, 0), bf), dot(x_down, w_in_all, (1, 0), bf)
    x_far = jnp.concatenate(after(far, parts[1], parts[3]))
    parts[2] = dot(x_far, w_in_all, (1, 0), bf)
    xs = [x_own, x_up, x_far, x_down]
    parts = [part.reshape(4, half, hidden) for part in parts]

    c_up, c_down = after((c_up, c_down), parts)
    c_far = jnp.concatenate([send(c_up[:2], Z_BY[3]), send(c_down[2:], Z_BY[1])])
    cs = [c.reshape(-1, 2 * width) for c in (c_own, c_up, c_far, c_down)]

    near = scatter_x(jnp.stack([parts[k] for k in (0, 1, 3)], axis=1))
    last = scatter_x(after(parts[2], near)[:, None])
    pre = jnp.concatenate([near[:2], last, near[2:]]) + b_in[None, None, :]
    act, slope = gelu_pair(pre)
    act_all = gather_x(act.astype(bf))

    d_parts = jnp.stack([dot(c, w_out_all, (1, 1), bf).reshape(4, half, hidden) for c in cs])
    d_parts, cs = after((d_parts, cs), act_all)
    d_act = swap_x(d_parts)
    c_mine = jnp.concatenate([c[:, :width] for c in cs])
    c_other = jnp.concatenate([c[:, width:] for c in cs])

    act_all = act_all.reshape(-1, hidden)
    cut = hidden // 2
    act_cuts = [act_all[:, :cut], act_all[:, cut:]]
    out_got = [send(dot(a, c_other, (0, 0), bf), CORE) for a in act_cuts]
    out_mine = [(dot(a, c_mine, (0, 0)) + got.astype(f32)).astype(bf) for a, got in zip(act_cuts, out_got)]
    out_deep = [send(mine, DEPTH) for mine in out_mine]

    d_act = jnp.sum(d_act.astype(f32), axis=0)
    d_pre_all = gather_x((d_act * slope).astype(bf))

    cut = width // 2
    x_mine = [jnp.concatenate([x[:, i * cut : (i + 1) * cut] for x in xs]) for i in (0, 1)]
    x_other = [jnp.concatenate([x[:, i * cut : (i + 1) * cut] for x in xs]) for i in (2, 3)]
    x_other[1] = jnp.concatenate([x_other[1], jnp.ones((x_other[1].shape[0], 16), bf)], axis=1)
    d_raw = after(d_pre_all, x_mine, x_other)
    d_pre_all = d_raw.swapaxes(0, 1)
    d_pre_rows = d_pre_all.reshape(-1, hidden)
    in_other = [dot(x, after(d_pre_rows, out_mine), (0, 0), bf) for x in x_other]
    in_got = [send(other, CORE) for other in in_other]
    far_rows = after(d_pre_rows[8 * half : 12 * half], in_other)
    far_share = dot(far_rows, w_in_all, (1, 1), bf)
    *shares, total = near_shares(after(d_raw, far_share), w_in_all)
    shares = [far_share, *shares]
    got = [send(share, Y_BY[k]) for share, k in zip(shares, (2, 1, 3))]
    in_got = after(in_got, *shares)
    out_deep = after(out_deep, *shares)
    d_w_out = jnp.concatenate(out_mine).astype(f32) + jnp.concatenate(out_deep).astype(f32)
    in_mine = [(dot(x, d_pre_rows, (0, 0)) + got[:cut].astype(f32)).astype(bf) for x, got in zip(x_mine, in_got)]
    bias = (in_other[1][cut:].astype(f32) + in_got[1][cut:].astype(f32)).astype(bf)
    in_both = [in_mine[0], jnp.concatenate([in_mine[1], bias])]
    in_deep = [send(mine, DEPTH) for mine in in_both]
    d_w_in = jnp.concatenate(in_mine).astype(f32) + jnp.concatenate([deep[:cut] for deep in in_deep]).astype(f32)

    for term in after(got, in_both):
        total = total + term.astype(f32)
    total = total.reshape(4, half, 2 * width)
    d_half = total[0]
    for term in after([send(total[j].astype(bf), Z_BY[j]) for j in range(1, 4)], in_deep):
        d_half = d_half + term.astype(f32)
    d_half = d_half.astype(bf)
    mine, got = d_half[:, :width], send(d_half[:, width:], CORE)
    first = jnp.where(core == 0, mine, got)
    second = jnp.where(core == 0, got, mine)
    d_normed = jnp.concatenate([first, second], axis=0)
    d_b_in = after(bias[0], d_normed, d_w_in, d_w_out).astype(f32) + in_deep[1][cut].astype(f32)
    return (d_normed, d_w_in, d_b_in, d_w_out)


def solution(mesh):
    placed = (
        P(("depth", "col"), "row"),
        P(("depth", "col")),
        P(("depth", "col"), "row"),
        P("row", "col"),
        P("col"),
        P("col", "row"),
    )
    return jax.shard_map(
        on_device,
        mesh=mesh,
        in_specs=placed,
        out_specs=(P(("depth", "col"), "row"), P("row", "col"), P("col"), P("col", "row")),
        check_vma=False,
    )
```

```python
import jax
import jax.numpy as jnp
from jax import lax
from jax.experimental import pallas as pl
from jax.sharding import PartitionSpec as P

D = 6144
AXES = ("depth", "row", "col")

coeff = 0.7978845608028654


def add_table_kernel(place_ref, freq_ref, normed_ref, out_ref):
    angle = place_ref[...] * freq_ref[...]
    even = lax.broadcasted_iota(jnp.int32, angle.shape, 1) % 2 == 0
    table = jnp.where(even, jnp.sin(angle), jnp.cos(angle))
    out_ref[...] = (normed_ref[...].astype(jnp.float32) + table).astype(out_ref.dtype)


def add_table(normed, positions, first):
    rows, width = normed.shape
    column = first + jnp.arange(width, dtype=jnp.int32)
    expo = (2 * (column // 2)).astype(jnp.float32) / jnp.float32(D)
    freq = jnp.power(jnp.float32(10000.0), -expo)
    tile = 16
    return pl.pallas_call(
        add_table_kernel,
        grid=(rows // tile,),
        in_specs=[
            pl.BlockSpec((tile, 1), lambda n: (n, 0)),
            pl.BlockSpec((1, width), lambda n: (0, 0)),
            pl.BlockSpec((tile, width), lambda n: (n, 0)),
        ],
        out_specs=pl.BlockSpec((tile, width), lambda n: (n, 0)),
        out_shape=jax.ShapeDtypeStruct(normed.shape, normed.dtype),
    )(positions.astype(jnp.float32)[:, None], freq[None, :], normed)


def gelu_pair(value):
    inner = coeff * (value + 0.044715 * value * value * value)
    slope = jnp.tanh(inner)
    out = 0.5 * value * (1.0 + slope)
    grad = 0.5 * (1.0 + slope) + 0.5 * value * (1.0 - slope * slope) * coeff * (
        1.0 + 3.0 * 0.044715 * value * value
    )
    return (out, grad)


def moves(shift):
    def index(d, x, c, z, y):
        return ((d % 2) * 8 + (x % 4) * 2 + c % 2) * 16 + (z % 4) * 4 + y % 4

    return [
        (index(d, x, c, z, y), index(*shift(d, x, c, z, y)))
        for d in range(2)
        for x in range(4)
        for c in range(2)
        for z in range(4)
        for y in range(4)
    ]


CORE = moves(lambda d, x, c, z, y: (d, x, c + 1, z, y))
DEPTH = moves(lambda d, x, c, z, y: (d + 1, x, c, z, y))
Y_BY = [moves(lambda d, x, c, z, y, k=k: (d, x, c, z, y + k)) for k in range(4)]
Z_BY = [moves(lambda d, x, c, z, y, j=j: (d, x, c, z + j, y)) for j in range(4)]
X_SETS = [[c + 2 * x for x in range(4)] for c in range(2)]

Y_SETS = [[z * 4 + y for y in range(4)] for z in range(4)]


def send(value, pairs):
    return lax.ppermute(value, AXES, pairs)


def dot(a, b, contract, kind=jnp.float32):
    return lax.dot_general(
        a, b, ((contract[:1], contract[1:]), ((), ())), preferred_element_type=jnp.float32
    ).astype(kind)


def share_kernel(d_ref, w_ref, *outs):
    for k, out in zip((2, 1, 3, 0), outs):
        rows = d_ref[:, k].reshape(out.shape[0], d_ref.shape[3])
        out[...] = lax.dot_general(
            rows, w_ref[...], (((1,), (1,)), ((), ())), preferred_element_type=jnp.float32
        ).astype(out.dtype)


def all_shares(d_pre, w):
    rows, wide, hidden = 4 * d_pre.shape[2], w.shape[0], w.shape[1]
    tile = 256
    return pl.pallas_call(
        share_kernel,
        grid=(wide // tile,),
        in_specs=[
            pl.BlockSpec(d_pre.shape, lambda n: (0, 0, 0, 0)),
            pl.BlockSpec((tile, hidden), lambda n: (n, 0)),
        ],
        out_specs=[pl.BlockSpec((rows, tile), lambda n: (0, n))] * 4,
        out_shape=[jax.ShapeDtypeStruct((rows, wide), kind) for kind in [d_pre.dtype] * 3 + [jnp.float32]],
        cost_estimate=pl.CostEstimate(
            flops=8 * rows * wide * hidden, bytes_accessed=2 * (d_pre.size + w.size + 5 * rows * wide), transcendentals=0
        ),
    )(d_pre, w)


def on_device(normed, positions, cotangent, w_in, b_in, w_out):
    bf, f32 = jnp.bfloat16, jnp.float32
    width = w_in.shape[0]
    hidden = w_in.shape[1]
    row = lax.axis_index("row")
    core = row % 2
    half = normed.shape[0] // 2

    def after(value, *others):
        return lax.optimization_barrier((value, *others))[0]

    def swap_x(value):
        return lax.all_to_all(value, "row", 0, 0, tiled=True, axis_index_groups=X_SETS)

    def scatter_x(part):
        return jnp.sum(swap_x(part).astype(f32), axis=0)

    def gather_x(own):
        return swap_x(jnp.broadcast_to(own[None], (4,) + own.shape))

    inputs = add_table(normed, positions, row * width)
    both = jnp.stack([inputs, cotangent])
    mine = lax.dynamic_slice_in_dim(both, core * half, half, 1)
    other = send(lax.dynamic_slice_in_dim(both, (1 - core) * half, half, 1), CORE)
    x_half = jnp.concatenate([mine[0], other[0]], axis=1)
    c_half = jnp.concatenate([mine[1], other[1]], axis=1)
    w_in_got = send(w_in, CORE)
    w_out_got = send(w_out, CORE)
    w_in_all = jnp.concatenate([w_in, w_in_got], axis=0)
    w_out_all = jnp.concatenate([w_out, w_out_got], axis=1)

    x_one, x_three, x_two = (send(x_half, Z_BY[4 - j]) for j in (1, 3, 2))
    c_four = jnp.broadcast_to(after(c_half, x_half)[None], (4,) + c_half.shape)
    c_four = lax.all_to_all(c_four, "col", 0, 0, tiled=True, axis_index_groups=Y_SETS)
    y = lax.axis_index("col") % 4
    c_own = lax.dynamic_slice_in_dim(jnp.concatenate([c_four, c_four]), y, 4, 0)
    x_own = jnp.concatenate([x_half, x_one, x_two, x_three])

    x_up, x_down = send(x_own, Y_BY[3]), send(x_own, Y_BY[1])
    c_own = after(c_own, x_own, w_in_got, w_out_got)
    c_up, c_down = send(c_own, Z_BY[3]), send(c_own, Z_BY[1])
    parts = [dot(x_own, w_in_all, (1, 0), bf), None, None, None]
    x_up, x_down = after((x_up, x_down), parts[0])
    rows = 2 * half
    far = [send(x_up[:rows], Y_BY[3]), send(x_down[rows:], Y_BY[1])]
    parts[1], parts[3] = dot(x_up, w_in_all, (1, 0), bf), dot(x_down, w_in_all, (1, 0), bf)
    x_far = jnp.concatenate(after(far, parts[1], parts[3]))
    parts[2] = dot(x_far, w_in_all, (1, 0), bf)
    xs = [x_own, x_up, x_far, x_down]
    parts = [part.reshape(4, half, hidden) for part in parts]

    c_up, c_down = after((c_up, c_down), parts)
    c_far = jnp.concatenate([send(c_up[:2], Z_BY[3]), send(c_down[2:], Z_BY[1])])
    cs = [c.reshape(-1, 2 * width) for c in (c_own, c_up, c_far, c_down)]

    near = scatter_x(jnp.stack([parts[k] for k in (0, 1, 3)], axis=1))
    last = scatter_x(after(parts[2], near)[:, None])
    pre = jnp.concatenate([near[:2], last, near[2:]]) + b_in[None, None, :]
    act, slope = gelu_pair(pre)
    act_all = gather_x(act.astype(bf))

    d_parts = jnp.stack([dot(c, w_out_all, (1, 1), bf).reshape(4, half, hidden) for c in cs])
    d_parts, cs = after((d_parts, cs), act_all)
    d_act = swap_x(d_parts)
    c_mine = jnp.concatenate([c[:, :width] for c in cs])
    c_other = jnp.concatenate([c[:, width:] for c in cs])

    act_all = act_all.reshape(-1, hidden)
    cut = hidden // 2
    act_cuts = [act_all[:, :cut], act_all[:, cut:]]
    out_got = [send(dot(a, c_other, (0, 0), bf), CORE) for a in act_cuts]
    out_mine = [(dot(a, c_mine, (0, 0)) + got.astype(f32)).astype(bf) for a, got in zip(act_cuts, out_got)]
    out_deep = [send(mine, DEPTH) for mine in out_mine]

    d_act = jnp.sum(d_act.astype(f32), axis=0)
    d_pre_all = gather_x((d_act * slope).astype(bf))

    cut = width // 2
    x_mine = [jnp.concatenate([x[:, i * cut : (i + 1) * cut] for x in xs]) for i in (0, 1)]
    x_other = [jnp.concatenate([x[:, i * cut : (i + 1) * cut] for x in xs]) for i in (2, 3)]
    x_other[1] = jnp.concatenate([x_other[1], jnp.ones((x_other[1].shape[0], 16), bf)], axis=1)
    d_raw = after(d_pre_all, x_mine, x_other)
    *shares, total = all_shares(d_raw, w_in_all)
    d_pre_all = after(d_raw, *shares).swapaxes(0, 1)
    d_pre_rows = d_pre_all.reshape(-1, hidden)
    in_other = [dot(x, after(d_pre_rows, out_mine), (0, 0), bf) for x in x_other]
    in_got = [send(other, CORE) for other in in_other]
    got = [send(share, Y_BY[k]) for share, k in zip(shares, (2, 1, 3))]
    in_got = after(in_got, *shares)
    out_deep = after(out_deep, *shares)
    d_w_out = jnp.concatenate(out_mine).astype(f32) + jnp.concatenate(out_deep).astype(f32)
    in_mine = [(dot(x, d_pre_rows, (0, 0)) + got[:cut].astype(f32)).astype(bf) for x, got in zip(x_mine, in_got)]
    bias = (in_other[1][cut:].astype(f32) + in_got[1][cut:].astype(f32)).astype(bf)
    in_both = [in_mine[0], jnp.concatenate([in_mine[1], bias])]
    in_deep = [send(mine, DEPTH) for mine in in_both]
    d_w_in = jnp.concatenate(in_mine).astype(f32) + jnp.concatenate([deep[:cut] for deep in in_deep]).astype(f32)

    for term in after(got, in_both):
        total = total + term.astype(f32)
    total = total.reshape(4, half, 2 * width)
    d_half = total[0]
    for term in after([send(total[j].astype(bf), Z_BY[j]) for j in range(1, 4)], in_deep):
        d_half = d_half + term.astype(f32)
    d_half = d_half.astype(bf)
    mine, got = d_half[:, :width], send(d_half[:, width:], CORE)
    first = jnp.where(core == 0, mine, got)
    second = jnp.where(core == 0, got, mine)
    d_normed = jnp.concatenate([first, second], axis=0)
    d_b_in = after(bias[0], d_normed, d_w_in, d_w_out).astype(f32) + in_deep[1][cut].astype(f32)
    return (d_normed, d_w_in, d_b_in, d_w_out)


def solution(mesh):
    placed = (
        P(("depth", "col"), "row"),
        P(("depth", "col")),
        P(("depth", "col"), "row"),
        P("row", "col"),
        P("col"),
        P("col", "row"),
    )
    return jax.shard_map(
        on_device,
        mesh=mesh,
        in_specs=placed,
        out_specs=(P(("depth", "col"), "row"), P("row", "col"), P("col"), P("col", "row")),
        check_vma=False,
    )
```

```python
import jax
import jax.numpy as jnp
from jax import lax
from jax.experimental import pallas as pl
from jax.sharding import PartitionSpec as P

D = 6144
AXES = ("depth", "row", "col")

coeff = 0.7978845608028654


def add_table_kernel(place_ref, freq_ref, normed_ref, out_ref):
    angle = place_ref[...] * freq_ref[...]
    even = lax.broadcasted_iota(jnp.int32, angle.shape, 1) % 2 == 0
    table = jnp.where(even, jnp.sin(angle), jnp.cos(angle))
    out_ref[...] = (normed_ref[...].astype(jnp.float32) + table).astype(out_ref.dtype)


def add_table(normed, positions, first):
    rows, width = normed.shape
    column = first + jnp.arange(width, dtype=jnp.int32)
    expo = (2 * (column // 2)).astype(jnp.float32) / jnp.float32(D)
    freq = jnp.power(jnp.float32(10000.0), -expo)
    tile = 16
    return pl.pallas_call(
        add_table_kernel,
        grid=(rows // tile,),
        in_specs=[
            pl.BlockSpec((tile, 1), lambda n: (n, 0)),
            pl.BlockSpec((1, width), lambda n: (0, 0)),
            pl.BlockSpec((tile, width), lambda n: (n, 0)),
        ],
        out_specs=pl.BlockSpec((tile, width), lambda n: (n, 0)),
        out_shape=jax.ShapeDtypeStruct(normed.shape, normed.dtype),
    )(positions.astype(jnp.float32)[:, None], freq[None, :], normed)


def gelu_pair(value):
    inner = coeff * (value + 0.044715 * value * value * value)
    slope = jnp.tanh(inner)
    out = 0.5 * value * (1.0 + slope)
    grad = 0.5 * (1.0 + slope) + 0.5 * value * (1.0 - slope * slope) * coeff * (
        1.0 + 3.0 * 0.044715 * value * value
    )
    return (out, grad)


def moves(shift):
    def index(d, x, c, z, y):
        return ((d % 2) * 8 + (x % 4) * 2 + c % 2) * 16 + (z % 4) * 4 + y % 4

    return [
        (index(d, x, c, z, y), index(*shift(d, x, c, z, y)))
        for d in range(2)
        for x in range(4)
        for c in range(2)
        for z in range(4)
        for y in range(4)
    ]


CORE = moves(lambda d, x, c, z, y: (d, x, c + 1, z, y))
DEPTH = moves(lambda d, x, c, z, y: (d + 1, x, c, z, y))
Y_BY = [moves(lambda d, x, c, z, y, k=k: (d, x, c, z, y + k)) for k in range(4)]
Z_BY = [moves(lambda d, x, c, z, y, j=j: (d, x, c, z + j, y)) for j in range(4)]
X_SETS = [[c + 2 * x for x in range(4)] for c in range(2)]

Y_SETS = [[z * 4 + y for y in range(4)] for z in range(4)]


def send(value, pairs):
    return lax.ppermute(value, AXES, pairs)


def dot(a, b, contract, kind=jnp.float32):
    return lax.dot_general(
        a, b, ((contract[:1], contract[1:]), ((), ())), preferred_element_type=jnp.float32
    ).astype(kind)


def share_kernel(d_ref, w_ref, *outs):
    for k, out in zip((2, 1, 3, 0), outs):
        rows = d_ref[:, k].reshape(out.shape[0], d_ref.shape[3])
        out[...] = lax.dot_general(
            rows, w_ref[...], (((1,), (1,)), ((), ())), preferred_element_type=jnp.float32
        ).astype(out.dtype)


def all_shares(d_pre, w):
    rows, wide, hidden = 4 * d_pre.shape[2], w.shape[0], w.shape[1]
    tile = 512
    return pl.pallas_call(
        share_kernel,
        grid=(wide // tile,),
        in_specs=[
            pl.BlockSpec(d_pre.shape, lambda n: (0, 0, 0, 0)),
            pl.BlockSpec((tile, hidden), lambda n: (n, 0)),
        ],
        out_specs=[pl.BlockSpec((rows, tile), lambda n: (0, n))] * 4,
        out_shape=[jax.ShapeDtypeStruct((rows, wide), kind) for kind in [d_pre.dtype] * 3 + [jnp.float32]],
        cost_estimate=pl.CostEstimate(
            flops=8 * rows * wide * hidden, bytes_accessed=2 * (d_pre.size + w.size + 5 * rows * wide), transcendentals=0
        ),
    )(d_pre, w)


def on_device(normed, positions, cotangent, w_in, b_in, w_out):
    bf, f32 = jnp.bfloat16, jnp.float32
    width = w_in.shape[0]
    hidden = w_in.shape[1]
    row = lax.axis_index("row")
    core = row % 2
    half = normed.shape[0] // 2

    def after(value, *others):
        return lax.optimization_barrier((value, *others))[0]

    def swap_x(value):
        return lax.all_to_all(value, "row", 0, 0, tiled=True, axis_index_groups=X_SETS)

    def scatter_x(part):
        return jnp.sum(swap_x(part).astype(f32), axis=0)

    def gather_x(own):
        return swap_x(jnp.broadcast_to(own[None], (4,) + own.shape))

    inputs = add_table(normed, positions, row * width)
    both = jnp.stack([inputs, cotangent])
    mine = lax.dynamic_slice_in_dim(both, core * half, half, 1)
    other = send(lax.dynamic_slice_in_dim(both, (1 - core) * half, half, 1), CORE)
    x_half = jnp.concatenate([mine[0], other[0]], axis=1)
    c_half = jnp.concatenate([mine[1], other[1]], axis=1)
    w_in_got = send(w_in, CORE)
    w_out_got = send(w_out, CORE)
    w_in_all = jnp.concatenate([w_in, w_in_got], axis=0)
    w_out_all = jnp.concatenate([w_out, w_out_got], axis=1)

    x_one, x_three, x_two = (send(x_half, Z_BY[4 - j]) for j in (1, 3, 2))
    c_four = jnp.broadcast_to(after(c_half, x_half)[None], (4,) + c_half.shape)
    c_four = lax.all_to_all(c_four, "col", 0, 0, tiled=True, axis_index_groups=Y_SETS)
    y = lax.axis_index("col") % 4
    c_own = lax.dynamic_slice_in_dim(jnp.concatenate([c_four, c_four]), y, 4, 0)
    x_own = jnp.concatenate([x_half, x_one, x_two, x_three])

    x_up, x_down = send(x_own, Y_BY[3]), send(x_own, Y_BY[1])
    c_own = after(c_own, x_own, w_in_got, w_out_got)
    c_up, c_down = send(c_own, Z_BY[3]), send(c_own, Z_BY[1])
    parts = [dot(x_own, w_in_all, (1, 0), bf), None, None, None]
    x_up, x_down = after((x_up, x_down), parts[0])
    rows = 2 * half
    far = [send(x_up[:rows], Y_BY[3]), send(x_down[rows:], Y_BY[1])]
    parts[1], parts[3] = dot(x_up, w_in_all, (1, 0), bf), dot(x_down, w_in_all, (1, 0), bf)
    x_far = jnp.concatenate(after(far, parts[1], parts[3]))
    parts[2] = dot(x_far, w_in_all, (1, 0), bf)
    xs = [x_own, x_up, x_far, x_down]
    parts = [part.reshape(4, half, hidden) for part in parts]

    c_up, c_down = after((c_up, c_down), parts)
    c_far = jnp.concatenate([send(c_up[:2], Z_BY[3]), send(c_down[2:], Z_BY[1])])
    cs = [c.reshape(-1, 2 * width) for c in (c_own, c_up, c_far, c_down)]

    near = scatter_x(jnp.stack([parts[k] for k in (0, 1, 3)], axis=1))
    last = scatter_x(after(parts[2], near)[:, None])
    pre = jnp.concatenate([near[:2], last, near[2:]]) + b_in[None, None, :]
    act, slope = gelu_pair(pre)
    act_all = gather_x(act.astype(bf))

    d_parts = jnp.stack([dot(c, w_out_all, (1, 1), bf).reshape(4, half, hidden) for c in cs])
    d_parts, cs = after((d_parts, cs), act_all)
    d_act = swap_x(d_parts)
    c_mine = jnp.concatenate([c[:, :width] for c in cs])
    c_other = jnp.concatenate([c[:, width:] for c in cs])

    act_all = act_all.reshape(-1, hidden)
    cut = hidden // 2
    act_cuts = [act_all[:, :cut], act_all[:, cut:]]
    out_got = [send(dot(a, c_other, (0, 0), bf), CORE) for a in act_cuts]
    out_mine = [(dot(a, c_mine, (0, 0)) + got.astype(f32)).astype(bf) for a, got in zip(act_cuts, out_got)]
    out_deep = [send(mine, DEPTH) for mine in out_mine]

    d_act = jnp.sum(d_act.astype(f32), axis=0)
    d_pre_all = gather_x((d_act * slope).astype(bf))

    cut = width // 2
    x_mine = [jnp.concatenate([x[:, i * cut : (i + 1) * cut] for x in xs]) for i in (0, 1)]
    x_other = [jnp.concatenate([x[:, i * cut : (i + 1) * cut] for x in xs]) for i in (2, 3)]
    x_other[1] = jnp.concatenate([x_other[1], jnp.ones((x_other[1].shape[0], 16), bf)], axis=1)
    d_raw = after(d_pre_all, x_mine, x_other)
    d_pre_all = d_raw.swapaxes(0, 1)
    d_pre_rows = d_pre_all.reshape(-1, hidden)
    in_other = [dot(x, after(d_pre_rows, out_mine), (0, 0), bf) for x in x_other]
    in_got = [send(other, CORE) for other in in_other]
    *shares, total = all_shares(after(d_raw, in_other), w_in_all)
    got = [send(share, Y_BY[k]) for share, k in zip(shares, (2, 1, 3))]
    in_got = after(in_got, *shares)
    out_deep = after(out_deep, *shares)
    d_w_out = jnp.concatenate(out_mine).astype(f32) + jnp.concatenate(out_deep).astype(f32)
    in_mine = [(dot(x, d_pre_rows, (0, 0)) + got[:cut].astype(f32)).astype(bf) for x, got in zip(x_mine, in_got)]
    bias = (in_other[1][cut:].astype(f32) + in_got[1][cut:].astype(f32)).astype(bf)
    in_both = [in_mine[0], jnp.concatenate([in_mine[1], bias])]
    in_deep = [send(mine, DEPTH) for mine in in_both]
    d_w_in = jnp.concatenate(in_mine).astype(f32) + jnp.concatenate([deep[:cut] for deep in in_deep]).astype(f32)

    for term in after(got, in_both):
        total = total + term.astype(f32)
    total = total.reshape(4, half, 2 * width)
    d_half = total[0]
    for term in after([send(total[j].astype(bf), Z_BY[j]) for j in range(1, 4)], in_deep):
        d_half = d_half + term.astype(f32)
    d_half = d_half.astype(bf)
    mine, got = d_half[:, :width], send(d_half[:, width:], CORE)
    first = jnp.where(core == 0, mine, got)
    second = jnp.where(core == 0, got, mine)
    d_normed = jnp.concatenate([first, second], axis=0)
    d_b_in = after(bias[0], d_normed, d_w_in, d_w_out).astype(f32) + in_deep[1][cut].astype(f32)
    return (d_normed, d_w_in, d_b_in, d_w_out)


def solution(mesh):
    placed = (
        P(("depth", "col"), "row"),
        P(("depth", "col")),
        P(("depth", "col"), "row"),
        P("row", "col"),
        P("col"),
        P("col", "row"),
    )
    return jax.shard_map(
        on_device,
        mesh=mesh,
        in_specs=placed,
        out_specs=(P(("depth", "col"), "row"), P("row", "col"), P("col"), P("col", "row")),
        check_vma=False,
    )
```
